256 devices in a mesh: tau: 32 (over z, x), ka: 8 (over y, core).
Axes of the slice: x: 4, y: 4, z: 8, core: 2. Of those that a mesh axis runs over, the one named last changes fastest.
Arguments:
- green_times: bfloat16 [32, 96, 256, 256], P('tau', 'ka'), may hold values from -16 to 16
- screened: bfloat16 [32, 96, 256, 256], P('tau', None, 'ka'), may hold values from -0.01953125 to 0.01953125
- bare_green: bfloat16 [32, 96, 2, 256, 256], P('tau', 'ka'), may hold values from -6 to 6
Outputs:
- mixed_green: bfloat16 [32, 96, 256, 256], P('tau', 'ka')
The draws below stay inside these ranges and needn't reach their ends.
All inputs are finite; a program needn't handle non-finite values.
Results may differ from the reference program's by a relative error of at most 0.025.
Values may be sent and summed in bfloat16 or wider, within the bound.
A program may use at most 128 MiB of HBM per device.

```python
import math
import jax
import jax.numpy as jnp
from jax import lax

NO = 256
KX = 6
KY = 4
KZ = 4
K = 96
TAU = 32
TURNS = 2


def draw_green_times(key, part):
    key = jax.random.fold_in(key, 11)
    time_rise = jnp.arange(TAU, dtype=jnp.float32)[:, None, None, None] / (TAU - 1)
    point_rise = jnp.arange(K, dtype=jnp.float32)[None, :, None, None] / (K - 1)
    growth = jnp.exp(math.log(3.0) * (time_rise + point_rise)) * 0.35
    value = jnp.clip(jax.random.normal(key, (TAU, K, NO, NO), jnp.float32), -5.0, 5.0) * growth
    return value.astype(jnp.bfloat16)


def level_of(stream_key, shape, cuts, least, high):
    level, own = 1.0, jax.random.fold_in(stream_key, 6)
    for dim, parts in cuts:
        steps = jnp.exp(jax.random.uniform(jax.random.fold_in(own, dim), (parts,), jnp.float32, least / len(cuts), high / len(cuts)))
        level = level * jnp.repeat(steps, shape[dim] // parts).reshape([-1 if axis == dim else 1 for axis in range(len(shape))])
    return level


def normal_values(rng, dims, spread, reach, shards=(), kind=jnp.bfloat16):
    result = spread * jax.random.normal(rng, dims, jnp.float32)
    if shards:
        result = result * level_of(rng, dims, shards, -0.22, 0.18)
    return jnp.clip(result, -reach, reach).astype(kind)


def setup_inputs(seed: int = 0) -> dict:
    streams_of = jax.random.split(jax.random.key(seed), 4)
    return {
        "green_times": draw_green_times(jax.random.fold_in(streams_of[3], 71), 0),
        "screened": normal_values(streams_of[1], (TAU, K, NO, NO), (0.36 / NO), 0.01953125, ((0, 32), (2, 8))),
        "bare_green": normal_values(streams_of[2], (TAU, K, 2, NO, NO), 1.0, 6.0, ((0, 32), (1, 8))),
    }


def hartley_table():
    count = KX * KY * KZ
    position = jnp.arange(count, dtype=jnp.int32)
    digit_one = position // (KY * KZ)
    digit_two = position // KZ % KY
    digit_three = position % KZ
    phase = (digit_one[:, None] * digit_one[None, :] * (KY * KZ) + digit_two[:, None] * digit_two[None, :] * (KX * KZ) + digit_three[:, None] * digit_three[None, :] * (KX * KY)) % count
    angle = phase.astype(jnp.float32) * (2.0 * math.pi / count)
    return ((jnp.cos(angle) + jnp.sin(angle)) / math.sqrt(count)).astype(jnp.bfloat16)

def time_tables(points):
    position = jnp.arange(points, dtype=jnp.int32)
    odd_index = 2 * position + 1
    phase = odd_index[:, None] * odd_index[None, :] % (4 * points)
    angle = phase.astype(jnp.float32) * (math.pi / (2 * points))
    factor = 1.0 / math.sqrt(points)
    return jnp.stack([jnp.cos(angle) * factor, jnp.sin(angle) * factor]).astype(jnp.bfloat16)

def rounded(value):
    return lax.optimization_barrier(value.astype(jnp.bfloat16)).astype(jnp.float32)

def batched(left, right):
    return jnp.einsum('nab,nbc->nac', left, right)

def reference(green_times, screened, bare_green):
    lattice = hartley_table().astype(jnp.float32)
    transform = time_tables(TAU).astype(jnp.float32)
    bare_by_k = jnp.moveaxis(bare_green, 1, 0)

    def cell_step(pair):
        block, screen = pair
        cells = jnp.einsum('rk,kab->rab', lattice, block.astype(jnp.float32))
        sigma_cells = rounded(-cells * screen.astype(jnp.float32))
        return jnp.einsum('kr,rab->kab', lattice, sigma_cells).astype(jnp.bfloat16)

    def point_step(pair):
        sigma_times, bare = pair
        sigma_freq = rounded(jnp.einsum('pnt,tab->pnab', transform, sigma_times.astype(jnp.float32)))
        real_part, imag_part = (sigma_freq[0], sigma_freq[1])
        bare_real = bare[:, 0].astype(jnp.float32)
        bare_imag = bare[:, 1].astype(jnp.float32)
        kernel_real = rounded(batched(bare_real, real_part) - batched(bare_imag, imag_part))
        kernel_imag = rounded(batched(bare_real, imag_part) + batched(bare_imag, real_part))
        dressed_real, dressed_imag = (bare_real, bare_imag)
        for turn in range(TURNS):
            new_real = bare_real + batched(kernel_real, dressed_real) - batched(kernel_imag, dressed_imag)
            new_imag = bare_imag + batched(kernel_real, dressed_imag) + batched(kernel_imag, dressed_real)
            dressed_real, dressed_imag = (rounded(new_real), rounded(new_imag))
        back = jnp.einsum('nt,nab->tab', transform[0], dressed_real) + jnp.einsum('nt,nab->tab', transform[1], dressed_imag)
        return back.astype(jnp.bfloat16)

    def apply(current):
        sigma_lattice = lax.map(cell_step, (current, screened))
        updated = lax.map(point_step, (jnp.moveaxis(sigma_lattice, 1, 0), bare_by_k))
        return jnp.moveaxis(updated, 0, 1)
    first_out = apply(green_times)
    start = green_times.astype(jnp.float32)
    first_res = first_out.astype(jnp.float32) - start
    relaxed = ((start + first_out.astype(jnp.float32)) * 0.5).astype(jnp.bfloat16)
    second_out = apply(relaxed)
    second_res = second_out.astype(jnp.float32) - relaxed.astype(jnp.float32)
    count = TAU * K * NO * NO
    first_mean = jnp.sum(first_res * first_res) / count
    cross_mean = jnp.sum(first_res * second_res) / count
    last_mean = jnp.sum(second_res * second_res) / count
    weight = (last_mean - cross_mean) / (first_mean - 2.0 * cross_mean + last_mean + 1e-06)
    mixed = weight * first_out.astype(jnp.float32) + (1.0 - weight) * second_out.astype(jnp.float32)
    return mixed.astype(jnp.bfloat16)
```

```python
import math

import jax
import jax.numpy as jnp
import numpy as np
from jax import lax
from jax.sharding import PartitionSpec as P

KX = 6
KY = 4
KZ = 4
TURNS = 2
F32 = jnp.float32
BF16 = jnp.bfloat16


def hartley_table():
    count = KX * KY * KZ
    position = np.arange(count)
    one = position // (KY * KZ)
    two = position // KZ % KY
    three = position % KZ
    phase = (
        one[:, None] * one[None, :] * (KY * KZ)
        + two[:, None] * two[None, :] * (KX * KZ)
        + three[:, None] * three[None, :] * (KX * KY)
    ) % count
    angle = phase * (2.0 * math.pi / count)
    return (np.cos(angle) + np.sin(angle)) / math.sqrt(count)


def time_tables(points):
    odd = 2 * np.arange(points) + 1
    angle = (odd[:, None] * odd[None, :] % (4 * points)) * (math.pi / (2 * points))
    factor = 1.0 / math.sqrt(points)
    return np.stack([np.cos(angle) * factor, np.sin(angle) * factor])


def product(left, right):
    return jnp.einsum("kab,kbc->kac", left, right, preferred_element_type=F32)


def dyson(bare_real, bare_imag, sigma_real, sigma_imag):
    kernel_real = (product(bare_real, sigma_real) - product(bare_imag, sigma_imag)).astype(BF16)
    kernel_imag = (product(bare_real, sigma_imag) + product(bare_imag, sigma_real)).astype(BF16)
    dressed_real, dressed_imag = bare_real, bare_imag
    for turn in range(TURNS):
        new_real = (
            bare_real.astype(F32)
            + product(kernel_real, dressed_real)
            - product(kernel_imag, dressed_imag)
        )
        new_imag = (
            bare_imag.astype(F32)
            + product(kernel_real, dressed_imag)
            + product(kernel_imag, dressed_real)
        )
        if turn < TURNS - 1:
            dressed_real, dressed_imag = new_real.astype(BF16), new_imag.astype(BF16)
    return new_real, new_imag


def per_device(green_times, screened, bare_green):
    points = lax.axis_size("tau")
    parts = lax.axis_size("ka")
    _, own_k, rows, cols = green_times.shape
    half = own_k // 2
    sub = rows // parts
    count = own_k * parts
    me = lax.axis_index("tau")
    low = me < points // 2

    order = np.arange(count).reshape(parts, 2, half).swapaxes(0, 1).reshape(-1)
    lattice = hartley_table()
    to_cells = jnp.asarray(lattice[:, order], BF16)
    to_points = jnp.asarray(lattice[order, :], BF16)
    table = time_tables(points)
    tables = jnp.asarray(table.transpose(1, 0, 2).reshape(2, points, points), BF16)

    def to_rows(block):
        spread = lax.all_to_all(block, "ka", split_axis=2, concat_axis=1, tiled=True)
        spread = spread.reshape(count, sub, cols).swapaxes(0, 1)
        return lax.all_to_all(spread, "tau", split_axis=0, concat_axis=0, tiled=True)

    def to_home(block):
        spread = lax.all_to_all(block, "tau", split_axis=0, concat_axis=0, tiled=True)
        spread = spread.reshape(sub, 2, parts * half, cols).transpose(1, 2, 0, 3)
        return lax.all_to_all(spread, "ka", split_axis=1, concat_axis=2, tiled=True)

    own, other = bare_green[0], None
    keep = jnp.where(low, own[:half], own[half:])
    send = jnp.where(low, own[half:], own[:half])
    other = lax.ppermute(send, "tau", [(i, points - 1 - i) for i in range(points)])

    start = to_rows(green_times.reshape(2, half, rows, cols))
    screen = lax.all_to_all(
        screened[0].swapaxes(0, 1), "tau", split_axis=0, concat_axis=0, tiled=True
    )

    def iterate(current):
        cells = jnp.einsum("rk,tkc->trc", to_cells, current, preferred_element_type=F32)
        sigma_cells = (-cells * screen.astype(F32)).astype(BF16)
        sigma = jnp.einsum(
            "kr,trc->tkc", to_points, sigma_cells, preferred_element_type=F32
        ).astype(BF16)
        sigma = sigma.reshape(points, 2, count // 2, cols)
        freq = jnp.einsum("hqt,thkc->hqkc", tables, sigma, preferred_element_type=F32).astype(BF16)
        freq = to_home(freq.reshape(points, count, cols))
        own_real, own_imag = dyson(keep[:, 0], keep[:, 1], freq[0], freq[1])
        other_real, other_imag = dyson(other[:, 0], other[:, 1], -freq[0], freq[1])
        dressed = jnp.stack([own_real - other_real, own_imag + other_imag]).astype(BF16)
        dressed = to_rows(dressed).reshape(2, points, count // 2, cols)
        back = jnp.einsum("hqt,hqkc->thkc", tables, dressed, preferred_element_type=F32)
        return back.astype(BF16).reshape(points, count, cols)

    first = iterate(start)
    begin = start.astype(F32)
    first_res = first.astype(F32) - begin
    relaxed = ((begin + first.astype(F32)) * 0.5).astype(BF16)
    second = iterate(relaxed)
    second_res = second.astype(F32) - relaxed.astype(F32)
    sums = jnp.stack(
        [
            jnp.sum(first_res * first_res),
            jnp.sum(first_res * second_res),
            jnp.sum(second_res * second_res),
        ]
    )
    total = float(points * count * rows * cols)
    means = lax.psum(sums, ("tau", "ka")) / total
    weight = (means[2] - means[1]) / (means[0] - 2.0 * means[1] + means[2] + 1e-06)
    mixed = (weight * first.astype(F32) + (1.0 - weight) * second.astype(F32)).astype(BF16)
    return to_home(mixed).reshape(1, own_k, rows, cols)


def solution(mesh):
    return jax.shard_map(
        per_device,
        mesh=mesh,
        in_specs=(
            P("tau", "ka", None, None),
            P("tau", None, "ka", None),
            P("tau", "ka", None, None, None),
        ),
        out_specs=P("tau", "ka", None, None),
        check_vma=False,
    )
```

```python
import functools
import math

import jax
import jax.numpy as jnp
import numpy as np
from jax import lax
from jax.experimental import pallas as pl
from jax.experimental.pallas import tpu as pltpu
from jax.sharding import PartitionSpec as P

KX = 6
KY = 4
KZ = 4
TURNS = 2
F32 = jnp.float32
BF16 = jnp.bfloat16
MESH = pl.DeviceIdType.MESH

TAU = 32
KA = 8
NO = 256
SUB = NO // KA
CHUNKS = 3
PAIR = 2
GROUP = PAIR * KA
COUNT = KX * KY * KZ
VMEM = pltpu.VMEM
LIMIT = 56 << 20


def hartley_table():
    count = COUNT
    position = np.arange(count)
    one = position // (KY * KZ)
    two = position // KZ % KY
    three = position % KZ
    phase = (
        one[:, None] * one[None, :] * (KY * KZ)
        + two[:, None] * two[None, :] * (KX * KZ)
        + three[:, None] * three[None, :] * (KX * KY)
    ) % count
    angle = phase * (2.0 * math.pi / count)
    return (np.cos(angle) + np.sin(angle)) / math.sqrt(count)


def time_tables(points):
    odd = 2 * np.arange(points) + 1
    angle = (odd[:, None] * odd[None, :] % (4 * points)) * (math.pi / (2 * points))
    factor = 1.0 / math.sqrt(points)
    return np.stack([np.cos(angle) * factor, np.sin(angle) * factor])


def tables():
    order = np.arange(COUNT).reshape(KA, 2, CHUNKS, PAIR).transpose(2, 1, 3, 0).reshape(-1)
    lattice = hartley_table()
    to_cells = lattice[:, order]
    to_points = lattice[order, :]
    times = time_tables(TAU).transpose(1, 0, 2).reshape(2, TAU, TAU)
    eye = np.eye(GROUP)
    to_freq = np.stack([np.kron(times[h], eye) for h in range(2)])
    to_time = np.stack([np.kron(times[h].T, eye) for h in range(2)])
    swap = np.eye(256).reshape(16, 16, 256).swapaxes(0, 1).reshape(256, 256)
    return [jnp.asarray(v, BF16) for v in (to_cells, to_points, to_freq, to_time, swap)]


class Place:
    def __init__(self):
        self.t = lax.axis_index("tau")
        self.a = lax.axis_index("ka")

    def tau_peer(self, d):
        row = lax.rem(self.t // 4 + d // 4, 8)
        return row * 4 + lax.rem(lax.rem(self.t, 4) + lax.rem(d, 4), 4)

    def ka_peer(self, d):
        return lax.rem(self.a + d, KA)

    def barrier(self):
        sem = pltpu.get_barrier_semaphore()

        def greet_tau(d, c):
            pl.semaphore_signal(
                sem, inc=1, device_id=(self.tau_peer(d), self.a), device_id_type=MESH
            )
            return c

        def greet_ka(d, c):
            pl.semaphore_signal(
                sem, inc=1, device_id=(self.t, self.ka_peer(d)), device_id_type=MESH
            )
            return c

        lax.fori_loop(1, TAU, greet_tau, 0)
        lax.fori_loop(1, KA, greet_ka, 0)
        pl.semaphore_wait(sem, TAU - 1 + KA - 1)

    def tau_send(self, src, dst, sems):
        def step(d, c):
            n = self.tau_peer(d)
            pltpu.make_async_remote_copy(
                src_ref=src.at[n],
                dst_ref=dst.at[self.t],
                send_sem=sems.at[0],
                recv_sem=sems.at[1],
                device_id=(n, self.a),
                device_id_type=MESH,
            ).start()
            return c

        lax.fori_loop(1, TAU, step, 0)
        dst[self.t] = src[self.t]

    def ka_send(self, src_of, dst, sems):
        def step(d, c):
            b = self.ka_peer(d)
            pltpu.make_async_remote_copy(
                src_ref=src_of(b),
                dst_ref=dst,
                send_sem=sems.at[0],
                recv_sem=sems.at[1],
                device_id=(self.t, b),
                device_id_type=MESH,
            ).start()
            return c

        lax.fori_loop(1, KA, step, 0)


def take(ref, sem):
    pltpu.make_async_copy(ref, ref, sem).wait()


def turn_over(swap, block):
    flat = block.reshape(256, NO)
    return jnp.dot(swap[...], flat, preferred_element_type=F32).astype(BF16).reshape(16, 16, NO)


def spread_out(swap, held, staged):
    for part in range(2):
        for uh in range(SUB // 16):
            rows = pl.ds(uh * 16, 16)
            block = jnp.stack([held[b, part, i, rows, :] for i in range(PAIR) for b in range(KA)])
            staged[rows, part] = turn_over(swap, block)


def gather_in(swap, held, staged):
    for part in range(2):
        for uh in range(SUB // 16):
            rows = pl.ds(uh * 16, 16)
            block = turn_over(swap, held[rows, part])
            for i in range(PAIR):
                for b in range(KA):
                    staged[b, part, i, rows, :] = block[i * KA + b]


def block_rows(b):
    return pl.ds(pl.multiple_of(b * SUB, SUB), SUB)


def spread_kernel(x, screened, bare, swap, out_x, out_w, out_bare, held, staged_x, staged_w, sems, swap_sems):
    place = Place()
    t, a = place.t, place.a
    place.barrier()
    mine = t // (TAU // 2)
    exchange = pltpu.make_async_remote_copy(
        src_ref=bare.at[1 - mine],
        dst_ref=out_bare,
        send_sem=swap_sems.at[0],
        recv_sem=swap_sems.at[1],
        device_id=(TAU - 1 - t, a),
        device_id_type=MESH,
    )
    for q in range(CHUNKS):
        points = pl.ds(q * PAIR, PAIR)
        place.ka_send(
            lambda b: x.at[:, points, block_rows(b), :], held.at[q, a], sems.at[q]
        )
        held[q, a] = x[:, points, block_rows(a), :]
    exchange.start()
    for q in range(CHUNKS):
        for cb in range(2):
            for uh in range(SUB // 16):
                cells = pl.ds(q * 32 + cb * 16, 16)
                rows = pl.ds(uh * 16, 16)
                staged_w[q, rows, pl.ds(cb * 16, 16), :] = turn_over(swap, screened[cells, rows, :])
        place.tau_send(staged_w.at[q], out_w.at[q], sems.at[CHUNKS + q])
    for q in range(CHUNKS):
        take(held.at[q, pl.ds(0, KA - 1)], sems.at[q, 1])
        spread_out(swap, held.at[q], staged_x.at[q])
        place.tau_send(staged_x.at[q], out_x.at[q], sems.at[2 * CHUNKS + q])
    for q in range(CHUNKS):
        take(out_w.at[q, pl.ds(0, TAU - 1)], sems.at[CHUNKS + q, 1])
        take(out_x.at[q, pl.ds(0, TAU - 1)], sems.at[2 * CHUNKS + q, 1])
    for q in range(CHUNKS):
        take(held.at[q, pl.ds(0, KA - 1)], sems.at[q, 0])
        take(out_w.at[q, pl.ds(0, TAU - 1)], sems.at[CHUNKS + q, 0])
        take(out_x.at[q, pl.ds(0, TAU - 1)], sems.at[2 * CHUNKS + q, 0])
    exchange.wait()


def mul(left, right):
    return jnp.dot(left, right, preferred_element_type=F32)


def dyson(bare_real, bare_imag, kernel_real, kernel_imag):
    dressed_real, dressed_imag = bare_real, bare_imag
    for turn in range(TURNS):
        new_real = (
            bare_real.astype(F32) + mul(kernel_real, dressed_real) - mul(kernel_imag, dressed_imag)
        )
        new_imag = (
            bare_imag.astype(F32) + mul(kernel_real, dressed_imag) + mul(kernel_imag, dressed_real)
        )
        dressed_real, dressed_imag = new_real.astype(BF16), new_imag.astype(BF16)
    return new_real, new_imag


def round_kernel(
    x, w, bare, other, to_cells, to_points, to_freq, to_time, swap,
    out_y, out_next,
    sigma, freq, freq_rows, home_stage, home, dressed, back, back_stage, back_rows, sems,
):
    place = Place()
    t, a = place.t, place.a
    mine = t // (TAU // 2)

    def lattice(i, c):
        block = x[:, i].reshape(COUNT, NO)
        cells = mul(to_cells[...], block)
        sigma_cells = (-cells * w[:, i].reshape(COUNT, NO).astype(F32)).astype(BF16)
        sigma[:, i] = mul(to_points[...], sigma_cells).astype(BF16).reshape(CHUNKS, 2, GROUP, NO)
        return c

    lax.fori_loop(0, TAU, lattice, 0, unroll=4)
    place.barrier()

    for q in range(CHUNKS):
        for h in range(2):
            block = sigma[q, :, h].reshape(TAU * GROUP, NO)
            value = mul(to_freq[h], block).astype(BF16)
            freq[q, pl.ds(h * 16, 16)] = value.reshape(16, 2, GROUP, NO)
        place.tau_send(freq.at[q], freq_rows.at[q], sems.at[q])

    def to_home(q):
        take(freq_rows.at[q, pl.ds(0, TAU - 1)], sems.at[q, 1])
        gather_in(swap, freq_rows.at[q], home_stage.at[q])
        target = home.at[q, :, :, block_rows(a), :]
        place.ka_send(lambda b: home_stage.at[q, b], target, sems.at[CHUNKS + q])
        home[q, :, :, block_rows(a), :] = home_stage[q, a]

    def solve(q):
        take(home_stage.at[q, pl.ds(0, KA - 1)], sems.at[CHUNKS + q, 1])

        def one(i, c):
            real, imag = home[q, 0, i], home[q, 1, i]
            point = q * PAIR + i
            br, bi = bare[mine, point, 0], bare[mine, point, 1]
            kr = (mul(br, real) - mul(bi, imag)).astype(BF16)
            ki = (mul(br, imag) + mul(bi, real)).astype(BF16)
            own_real, own_imag = dyson(br, bi, kr, ki)
            br, bi = other[point, 0], other[point, 1]
            kr = (-(mul(br, real) + mul(bi, imag))).astype(BF16)
            ki = (mul(br, imag) - mul(bi, real)).astype(BF16)
            other_real, other_imag = dyson(br, bi, kr, ki)
            dressed[q, 0, i] = (own_real - other_real).astype(BF16)
            dressed[q, 1, i] = (own_imag + other_imag).astype(BF16)
            return c

        lax.fori_loop(0, PAIR, one, 0)
        place.ka_send(
            lambda b: dressed.at[q, :, :, block_rows(b), :],
            back.at[q, a],
            sems.at[2 * CHUNKS + q],
        )
        back[q, a] = dressed[q, :, :, block_rows(a), :]

    def to_rows(q):
        take(back.at[q, pl.ds(0, KA - 1)], sems.at[2 * CHUNKS + q, 1])
        spread_out(swap, back.at[q], back_stage.at[q])
        place.tau_send(back_stage.at[q], back_rows.at[q], sems.at[3 * CHUNKS + q])

    to_home(0)
    to_home(1)
    solve(0)
    to_home(2)
    to_rows(0)
    solve(1)
    to_rows(1)
    solve(2)
    to_rows(2)

    for q in range(CHUNKS):
        take(back_rows.at[q, pl.ds(0, TAU - 1)], sems.at[3 * CHUNKS + q, 1])
        for h in range(2):
            block = back_rows[q, pl.ds(h * 16, 16)].reshape(TAU * GROUP, NO)
            value = mul(to_time[h], block).astype(BF16).reshape(TAU, GROUP, NO)
            out_y[q, :, h] = value
            half = (x[q, :, h].astype(F32) + value.astype(F32)) * 0.5
            out_next[q, :, h] = half.astype(BF16)
    for q in range(CHUNKS):
        take(freq_rows.at[q, pl.ds(0, TAU - 1)], sems.at[q, 0])
        take(home_stage.at[q, pl.ds(0, KA - 1)], sems.at[CHUNKS + q, 0])
        take(back.at[q, pl.ds(0, KA - 1)], sems.at[2 * CHUNKS + q, 0])
        take(back_rows.at[q, pl.ds(0, TAU - 1)], sems.at[3 * CHUNKS + q, 0])


def finish_kernel(
    x0, y0, x1, y1, swap, out,
    sums, tau_sums, part_sums, ka_sums, mixed, mixed_rows, home_stage, sems, sum_sems,
):
    place = Place()
    t, a = place.t, place.a

    def residuals(i, c):
        begin, first = x0[:, i].astype(F32), y0[:, i].astype(F32)
        relaxed, second = x1[:, i].astype(F32), y1[:, i].astype(F32)
        r0 = (first - begin).reshape(COUNT // 8, 8, NO)
        r1 = (second - relaxed).reshape(COUNT // 8, 8, NO)
        return (
            c[0] + jnp.sum(r0 * r0, axis=0),
            c[1] + jnp.sum(r0 * r1, axis=0),
            c[2] + jnp.sum(r1 * r1, axis=0),
        )

    zero = jnp.zeros((8, NO), F32)
    total = lax.fori_loop(0, TAU, residuals, (zero, zero, zero))
    sums[...] = jnp.stack([v[:, :128] + v[:, 128:] for v in total])
    place.barrier()

    def tau_step(d, c):
        pltpu.make_async_remote_copy(
            src_ref=sums,
            dst_ref=tau_sums.at[t],
            send_sem=sum_sems.at[0, 0],
            recv_sem=sum_sems.at[0, 1],
            device_id=(place.tau_peer(d), a),
            device_id_type=MESH,
        ).start()
        return c

    lax.fori_loop(1, TAU, tau_step, 0)
    tau_sums[t] = sums[...]
    take(tau_sums.at[pl.ds(0, TAU - 1)], sum_sems.at[0, 1])
    part_sums[...] = jnp.sum(tau_sums[...], axis=0)
    place.ka_send(lambda b: part_sums, ka_sums.at[a], sum_sems.at[1])
    ka_sums[a] = part_sums[...]
    take(ka_sums.at[pl.ds(0, KA - 1)], sum_sems.at[1, 1])
    whole = jnp.sum(ka_sums[...], axis=0)
    means = [jnp.sum(whole[j]) * (1.0 / (TAU * COUNT * NO * NO)) for j in range(3)]
    top = jnp.full((GROUP, NO), means[2] - means[1], F32)
    bottom = jnp.full((GROUP, NO), means[0] - 2.0 * means[1] + means[2] + 1e-06, F32)
    weight = top / bottom
    rest = 1.0 - weight

    for q in range(CHUNKS):

        def mix(i, c):
            value = weight * y0[q, i].astype(F32) + rest * y1[q, i].astype(F32)
            mixed[q, i] = value.astype(BF16)
            return c

        lax.fori_loop(0, TAU, mix, 0)
        place.tau_send(mixed.at[q], mixed_rows.at[q], sems.at[q])
    for q in range(CHUNKS):
        take(mixed_rows.at[q, pl.ds(0, TAU - 1)], sems.at[q, 1])
        gather_in(swap, mixed_rows.at[q], home_stage.at[q])
        points = pl.ds(q * PAIR, PAIR)
        place.ka_send(
            lambda b: home_stage.at[q, b],
            out.at[:, points, block_rows(a), :],
            sems.at[CHUNKS + q],
        )
        out[:, points, block_rows(a), :] = home_stage[q, a]
    for q in range(CHUNKS):
        take(home_stage.at[q, pl.ds(0, KA - 1)], sems.at[CHUNKS + q, 1])
    for q in range(CHUNKS):
        take(mixed_rows.at[q, pl.ds(0, TAU - 1)], sems.at[q, 0])
        take(home_stage.at[q, pl.ds(0, KA - 1)], sems.at[CHUNKS + q, 0])
    take(tau_sums.at[pl.ds(0, TAU - 1)], sum_sems.at[0, 0])
    take(ka_sums.at[pl.ds(0, KA - 1)], sum_sems.at[1, 0])


ROWS_X = (CHUNKS, TAU, 2, GROUP, NO)
ROWS_W = (CHUNKS, TAU, 2 * GROUP, NO)
HELD = (CHUNKS, KA, 2, PAIR, SUB, NO)
HOME = (CHUNKS, 2, PAIR, NO, NO)


def call(kernel, collective, outs, operands, scratch, anys=(), any_outs=()):
    place = lambda j, held: pl.BlockSpec(memory_space=pl.ANY if j in held else VMEM)
    return pl.pallas_call(
        kernel,
        out_shape=[jax.ShapeDtypeStruct(s, BF16) for s in outs],
        in_specs=[place(j, anys) for j in range(len(operands))],
        out_specs=[place(j, any_outs) for j in range(len(outs))],
        scratch_shapes=scratch,
        compiler_params=pltpu.CompilerParams(
            collective_id=collective, has_side_effects=True, vmem_limit_bytes=LIMIT
        ),
    )(*operands)


def per_device(green_times, screened, bare_green):
    to_cells, to_points, to_freq, to_time, swap = tables()
    half = CHUNKS * PAIR
    bare = bare_green.reshape(2, half, 2, NO, NO)
    buffer = lambda s: pltpu.VMEM(s, BF16)
    dma = pltpu.SemaphoreType.DMA
    x0, w, other = call(
        spread_kernel,
        0,
        [ROWS_X, ROWS_W, bare.shape[1:]],
        [green_times.reshape(2, half, NO, NO), screened[0], bare, swap],
        [buffer(HELD), buffer(ROWS_X), buffer(ROWS_W), dma((3 * CHUNKS, 2)), dma((2,))],
        anys=(2,),
        any_outs=(2,),
    )

    def one_round(x):
        return call(
            round_kernel,
            1,
            [ROWS_X, ROWS_X],
            [x, w, bare, other, to_cells, to_points, to_freq, to_time, swap],
            [
                buffer(ROWS_X), buffer(ROWS_X), buffer(ROWS_X), buffer(HELD), buffer(HOME),
                buffer(HOME), buffer(HELD), buffer(ROWS_X), buffer(ROWS_X), dma((4 * CHUNKS, 2)),
            ],
        )

    y0, x1 = one_round(x0)
    y1, _ = one_round(x1)
    (out,) = call(
        finish_kernel,
        2,
        [(2, half, NO, NO)],
        [x0, y0, x1, y1, swap],
        [
            pltpu.VMEM((3, 8, 128), F32), pltpu.VMEM((TAU, 3, 8, 128), F32),
            pltpu.VMEM((3, 8, 128), F32), pltpu.VMEM((KA, 3, 8, 128), F32),
            buffer(ROWS_X), buffer(ROWS_X), buffer(HELD), dma((2 * CHUNKS, 2)), dma((2, 2)),
        ],
    )
    return out.reshape(green_times.shape)


def solution(mesh):
    return jax.shard_map(
        per_device,
        mesh=mesh,
        in_specs=(
            P("tau", "ka", None, None),
            P("tau", None, "ka", None),
            P("tau", "ka", None, None, None),
        ),
        out_specs=P("tau", "ka", None, None),
        check_vma=False,
    )
```

```python
import math

import jax
import jax.numpy as jnp
import numpy as np
from jax import lax
from jax.experimental import pallas as pl
from jax.experimental.pallas import tpu as pltpu
from jax.sharding import PartitionSpec as P

KX = 6
KY = 4
KZ = 4
TURNS = 2
F32 = jnp.float32
BF16 = jnp.bfloat16
MESH = pl.DeviceIdType.MESH

Z, X, Y, C = 8, 4, 4, 2
TAU = Z * X
KA = Y * C
LAYER = X * KA
NO = 256
SUB = NO // KA
STEPS = 3
JUMP = 4
COUNT = KX * KY * KZ
VMEM = pltpu.VMEM
LIMIT = 60 << 20


def hartley_table():
    position = np.arange(COUNT)
    one = position // (KY * KZ)
    two = position // KZ % KY
    three = position % KZ
    phase = (
        one[:, None] * one[None, :] * (KY * KZ)
        + two[:, None] * two[None, :] * (KX * KZ)
        + three[:, None] * three[None, :] * (KX * KY)
    ) % COUNT
    angle = phase * (2.0 * math.pi / COUNT)
    return (np.cos(angle) + np.sin(angle)) / math.sqrt(COUNT)


def time_tables(points):
    odd = 2 * np.arange(points) + 1
    angle = (odd[:, None] * odd[None, :] % (4 * points)) * (math.pi / (2 * points))
    factor = 1.0 / math.sqrt(points)
    return np.stack([np.cos(angle) * factor, np.sin(angle) * factor])


def tables():
    order = np.arange(COUNT).reshape(Y, Z, STEPS).transpose(2, 1, 0).reshape(-1)
    lattice = hartley_table()
    to_cells = lattice[:, order]
    to_points = lattice[order, :]
    x, c, i = np.meshgrid(np.arange(X), np.arange(C), np.arange(2), indexing="ij")
    pairs = ((c + 2 * i) * X + x).reshape(-1)
    times = time_tables(TAU)[:, pairs, :]
    to_freq = np.einsum("pmt,kl,uv->kmputlv", times, np.eye(2), np.eye(8)).reshape(512, 512)
    swap = np.eye(256).reshape(16, 16, 256).swapaxes(0, 1).reshape(256, 256)
    leave = np.eye(256).reshape(2, 8, 16, 256).transpose(0, 2, 1, 3).reshape(256, 256)
    homing = np.eye(256).reshape(2, 16, 8, 256).transpose(1, 0, 2, 3).reshape(256, 256)
    arrays = (to_cells, to_points, to_freq, to_freq.T, swap, leave, leave.T, homing)
    return [jnp.asarray(v, BF16) for v in arrays]


def take(ref, sem):
    pltpu.make_async_copy(ref, ref, sem).wait()


def mul(left, right):
    return jnp.dot(left, right, preferred_element_type=F32)


def permute(matrix, block):
    return mul(matrix[...], block.reshape(256, NO)).astype(BF16).reshape(16, 16, NO)


def block_rows(b):
    return pl.ds(pl.multiple_of(b * SUB, SUB), SUB)


def dyson(bare_real, bare_imag, kernel_real, kernel_imag):
    dressed_real, dressed_imag = bare_real, bare_imag
    for turn in range(TURNS):
        new_real = (
            bare_real.astype(F32) + mul(kernel_real, dressed_real) - mul(kernel_imag, dressed_imag)
        )
        new_imag = (
            bare_imag.astype(F32) + mul(kernel_real, dressed_imag) + mul(kernel_imag, dressed_real)
        )
        dressed_real, dressed_imag = new_real.astype(BF16), new_imag.astype(BF16)
    return new_real, new_imag


def kernel(
    x_home, screened, bare, to_cells, to_points, to_freq, to_time, swap, leave, enter, homing,
    out,
    x_parts, x, w, y, sigma, sigma_out, sigma_in, freq_out, freq_in, dressed_out, dressed_in,
    time_out, time_in, home_out, home, bare_in, partial, sums, tau_sums, part_sums, ka_sums,
    x_sems, bare_sems, leave_sems, sigma_sems, freq_sems, dressed_sems, time_sems, home_sems, sum_sems,
):
    t, a = lax.axis_index("tau"), lax.axis_index("ka")
    my_z, my_x = t // X, lax.rem(t, X)
    my_y, my_c = a // C, lax.rem(a, C)

    def send(src, dst, sems, device):
        pltpu.make_async_remote_copy(
            src_ref=src, dst_ref=dst, send_sem=sems.at[0], recv_sem=sems.at[1],
            device_id=device, device_id_type=MESH,
        ).start()

    def loop(count, body):
        def step(d, c):
            body(d)
            return c

        lax.fori_loop(1, count, step, 0)

    def tau_peer(d):
        z, other_x = lax.rem(my_z + d // X, Z), lax.rem(my_x + lax.rem(d, X), X)
        return z, other_x, (z * X + other_x, a)

    def layer_peer(d):
        other_x, b = lax.rem(my_x + d // KA, X), lax.rem(a + lax.rem(d, KA), KA)
        return other_x, b, (my_z * X + other_x, b)

    def ka_peer(d):
        b = lax.rem(a + d, KA)
        return b, (t, b)

    low = my_z < Z // 2
    row = jnp.where(low, my_z, Z - 1 - my_z)
    goal_x = jnp.where(low, my_x, X - 1 - my_x)
    goal_i, goal_f = row // 2, jnp.where(low, 0, 1)
    goal_a = my_y * C + lax.rem(row, 2)

    def goal(jump):
        z = my_c * JUMP + jump
        here = (z == my_z) & (goal_x == my_x) & (goal_a == a)
        return here, (z * X + goal_x, goal_a)

    def origin(i, f):
        z = my_c + 2 * i if f == 0 else Z - 1 - (my_c + 2 * i)
        other_x = my_x if f == 0 else X - 1 - my_x
        b = my_y * C + my_z // JUMP
        here = (z == my_z) & (other_x == my_x) & (b == a)
        return here, (z * X + other_x, b)

    barrier = pltpu.get_barrier_semaphore()

    def greet(device):
        pl.semaphore_signal(barrier, inc=1, device_id=device, device_id_type=MESH)

    loop(TAU, lambda d: greet(tau_peer(d)[2]))
    loop(LAYER, lambda d: greet(layer_peer(d)[2]))
    for i in range(2):
        for f in range(2):
            here, device = origin(i, f)
            pl.when(jnp.logical_not(here))(lambda device=device: greet(device))
    greeters = TAU - 1 + LAYER - 1
    for jump in range(JUMP):
        greeters += jnp.where(goal(jump)[0], 0, 1)
    pl.semaphore_wait(barrier, greeters)

    for s in range(STEPS):

        def spread(d):
            b, device = ka_peer(d)
            send(x_home.at[:, s, block_rows(b), :], x_parts.at[s, a], x_sems.at[s], device)

        loop(KA, spread)
        x_parts[s, a] = x_home[:, s, block_rows(a), :]
    for s in range(STEPS):
        for jump in range(JUMP):
            here, device = goal(jump)
            arrived = bare_sems.at[s, goal_i, goal_f]
            target = bare_in.at[s, goal_i, goal_f]

            @pl.when(jnp.logical_not(here))
            def _():
                pltpu.make_async_remote_copy(
                    src_ref=bare.at[jump, s], dst_ref=target, send_sem=leave_sems.at[s, jump],
                    recv_sem=arrived, device_id=device, device_id_type=MESH,
                ).start()

            @pl.when(here)
            def _():
                pltpu.make_async_copy(bare.at[jump, s], target, arrived).start()

    for cells in range(COUNT // 16):
        for uh in range(2):
            rows, columns = pl.ds(uh * 16, 16), pl.ds(cells * 16, 16)
            w[rows, columns, :] = permute(swap, screened[columns, rows, :])
    for s in range(STEPS):
        take(x_parts.at[s, pl.ds(0, KA - 1)], x_sems.at[s, 1])
        for c in range(C):
            for uh in range(2):
                rows = pl.ds(uh * 16, 16)
                block = jnp.stack(
                    [x_parts[s, b * C + c, j, rows, :] for j in range(JUMP) for b in range(Y)]
                )
                x[0, s, rows, pl.ds(c * 16, 16), :] = permute(swap, block)

    def one_round(turn):
        def lattice(u, c):
            block = x[turn, :, u].reshape(COUNT, NO)
            cells = mul(to_cells[...], block)
            sigma_cells = (-cells * w[u].astype(F32)).astype(BF16)
            sigma[:, u] = mul(to_points[...], sigma_cells).astype(BF16).reshape(STEPS, 32, NO)
            return c

        lax.fori_loop(0, SUB, lattice, 0, unroll=4)
        if turn:
            for s in range(STEPS):
                take(sigma_in.at[0, s, pl.ds(0, TAU - 1)], sigma_sems.at[0, s, 0])
                take(freq_in.at[0, s, pl.ds(0, LAYER - 1)], freq_sems.at[0, s, 0])
                take(freq_in.at[0, s, pl.ds(0, LAYER - 1)], dressed_sems.at[0, s, 0])
                take(sigma_in.at[0, s, pl.ds(0, TAU - 1)], time_sems.at[0, s, 0])
                take(home_out.at[s, pl.ds(0, KA - 1)], home_sems.at[0, s, 0])

        for s in range(STEPS):
            for zh in range(2):
                for xh in range(2):
                    block = sigma[s, pl.ds(xh * 16, 16), pl.ds(zh * 16, 16), :]
                    block = permute(leave, block).reshape(2, 4, 2, 16, NO)
                    for j in range(2):
                        sigma_out[s, pl.ds(zh * 4, 4), xh * 2 + j] = block[j]

            def part(d):
                z, other_x, device = tau_peer(d)
                send(
                    sigma_out.at[s, z, other_x], sigma_in.at[turn, s, t],
                    sigma_sems.at[turn, s], device,
                )

            loop(TAU, part)
            sigma_in[turn, s, t] = sigma_out[s, my_z, my_x]

        def to_frequencies(s):
            take(sigma_in.at[turn, s, pl.ds(0, TAU - 1)], sigma_sems.at[turn, s, 1])
            for j in range(2):
                block = sigma_in[turn, s, :, j].reshape(512, NO)
                value = mul(to_freq[...], block).astype(BF16)
                freq_out[s, pl.ds(j * 2, 2)] = value.reshape(2, X * C, 2, 16, NO)

            def part(d):
                other_x, b, device = layer_peer(d)
                send(
                    freq_out.at[s, b // C, other_x * C + lax.rem(b, C)],
                    freq_in.at[turn, s, a * X + my_x],
                    freq_sems.at[turn, s], device,
                )

            loop(LAYER, part)
            freq_in[turn, s, a * X + my_x] = freq_out[s, my_y, my_x * C + my_c]

        def solve(s):
            take(freq_in.at[turn, s, pl.ds(0, LAYER - 1)], freq_sems.at[turn, s, 1])
            if turn == 0:
                for i in range(2):
                    for f in range(2):
                        take(bare_in.at[s, i, f], bare_sems.at[s, i, f])

            def one(i, c):
                both = freq_in[turn, s, :, i].astype(F32).reshape(LAYER, 2, 8, NO)
                real = both[:, 0].reshape(NO, NO).astype(BF16)
                imag = both[:, 1].reshape(NO, NO).astype(BF16)
                br, bi = bare_in[s, i, 0, 0], bare_in[s, i, 0, 1]
                kr = (mul(br, real) - mul(bi, imag)).astype(BF16)
                ki = (mul(br, imag) + mul(bi, real)).astype(BF16)
                low_real, low_imag = dyson(br, bi, kr, ki)
                br, bi = bare_in[s, i, 1, 0], bare_in[s, i, 1, 1]
                kr = (-(mul(br, real) + mul(bi, imag))).astype(BF16)
                ki = (mul(br, imag) - mul(bi, real)).astype(BF16)
                high_real, high_imag = dyson(br, bi, kr, ki)
                real = (low_real - high_real).reshape(LAYER, 1, 8, NO)
                imag = (low_imag + high_imag).reshape(LAYER, 1, 8, NO)
                both = jnp.concatenate([real, imag], axis=1).reshape(LAYER, 16, NO)
                dressed_out[s, :, i] = both.astype(BF16)
                return c

            lax.fori_loop(0, 2, one, 0)

            def part(d):
                other_x, b, device = layer_peer(d)
                send(
                    dressed_out.at[s, b * X + other_x],
                    dressed_in.at[turn, s, my_y, my_x * C + my_c],
                    dressed_sems.at[turn, s], device,
                )

            loop(LAYER, part)
            dressed_in[turn, s, my_y, my_x * C + my_c] = dressed_out[s, a * X + my_x]

        def to_times(s):
            take(freq_in.at[turn, s, pl.ds(0, LAYER - 1)], dressed_sems.at[turn, s, 1])
            for j in range(2):
                block = dressed_in[turn, s, pl.ds(j * 2, 2)].reshape(512, NO)
                value = mul(to_time[...], block).astype(BF16)
                time_out[s, :, j] = value.reshape(TAU, 16, NO)

            def part(d):
                z, other_x, device = tau_peer(d)
                send(
                    time_out.at[s, z * X + other_x], time_in.at[turn, s, my_z, my_x],
                    time_sems.at[turn, s], device,
                )

            loop(TAU, part)
            time_in[turn, s, my_z, my_x] = time_out[s, t]

        def finish(s):
            take(sigma_in.at[turn, s, pl.ds(0, TAU - 1)], time_sems.at[turn, s, 1])
            for zh in range(2):
                for xh in range(2):
                    rows, columns = pl.ds(xh * 16, 16), pl.ds(zh * 16, 16)
                    block = jnp.stack(
                        [time_in[turn, s, pl.ds(zh * 4, 4), xh * 2 + j] for j in range(2)]
                    )
                    value = permute(enter, block)
                    old = x[turn, s, rows, columns, :].astype(F32)
                    if turn == 0:
                        y[s, rows, columns, :] = value
                        x[1, s, rows, columns, :] = ((old + value.astype(F32)) * 0.5).astype(BF16)
                    else:
                        begin = x[0, s, rows, columns, :].astype(F32)
                        first = y[s, rows, columns, :].astype(F32) - begin
                        second = value.astype(F32) - old
                        for j, term in enumerate((first * first, first * second, second * second)):
                            partial[j] += jnp.sum(term.reshape(32, 8, NO), axis=0)
                    value = permute(homing, block)
                    for j in range(JUMP):
                        for b in range(Y):
                            home_out[s, b * C + zh, j, rows, :] = value[j * Y + b]

            def part(d):
                b, device = ka_peer(d)
                send(
                    home_out.at[s, b], home.at[turn, :, s, block_rows(a), :],
                    home_sems.at[turn, s], device,
                )

            loop(KA, part)
            home[turn, :, s, block_rows(a), :] = home_out[s, a]

        to_frequencies(0)
        to_frequencies(1)
        solve(0)
        to_frequencies(2)
        to_times(0)
        solve(1)
        to_times(1)
        solve(2)
        to_times(2)
        for s in range(STEPS):
            finish(s)

    partial[...] = jnp.zeros_like(partial)
    one_round(0)
    one_round(1)

    index = lax.broadcasted_iota(jnp.int32, (8, 128), 0)
    tile = jnp.zeros((8, 128), F32)
    for j in range(3):
        line = jnp.sum(partial[j], axis=0, keepdims=True)
        line = line[:, :128] + line[:, 128:]
        tile = jnp.where(index == j, jnp.broadcast_to(line, (8, 128)), tile)
    sums[...] = tile
    loop(TAU, lambda d: send(sums, tau_sums.at[t], sum_sems.at[0], tau_peer(d)[2]))
    tau_sums[t] = tile
    take(tau_sums.at[pl.ds(0, TAU - 1)], sum_sems.at[0, 1])
    part_sums[...] = jnp.sum(tau_sums[...], axis=0)
    loop(KA, lambda d: send(part_sums, ka_sums.at[a], sum_sems.at[1], ka_peer(d)[1]))
    ka_sums[a] = part_sums[...]
    take(ka_sums.at[pl.ds(0, KA - 1)], sum_sems.at[1, 1])
    whole = jnp.sum(ka_sums[...], axis=0)
    means = [
        jnp.sum(jnp.where(index == j, whole, 0.0)) * (1.0 / (TAU * COUNT * NO * NO))
        for j in range(3)
    ]
    top = jnp.full((NO, NO), means[2] - means[1], F32)
    weight = top / (means[0] - 2.0 * means[1] + means[2] + 1e-06)
    rest = 1.0 - weight
    for s in range(STEPS):
        for turn in range(2):
            take(home_out.at[s, pl.ds(0, KA - 1)], home_sems.at[turn, s, 1])
        for j in range(JUMP):
            value = weight * home[0, j, s].astype(F32) + rest * home[1, j, s].astype(F32)
            out[j, s] = value.astype(BF16)

    for s in range(STEPS):
        take(x_parts.at[s, pl.ds(0, KA - 1)], x_sems.at[s, 0])
        take(sigma_in.at[1, s, pl.ds(0, TAU - 1)], sigma_sems.at[1, s, 0])
        take(freq_in.at[1, s, pl.ds(0, LAYER - 1)], freq_sems.at[1, s, 0])
        take(freq_in.at[1, s, pl.ds(0, LAYER - 1)], dressed_sems.at[1, s, 0])
        take(sigma_in.at[1, s, pl.ds(0, TAU - 1)], time_sems.at[1, s, 0])
        take(home_out.at[s, pl.ds(0, KA - 1)], home_sems.at[1, s, 0])
        for jump in range(JUMP):
            here, _ = goal(jump)

            @pl.when(jnp.logical_not(here))
            def _():
                take(bare.at[jump, s], leave_sems.at[s, jump])

    take(tau_sums.at[pl.ds(0, TAU - 1)], sum_sems.at[0, 0])
    take(ka_sums.at[pl.ds(0, KA - 1)], sum_sems.at[1, 0])


def per_device(green_times, screened, bare_green):
    operands = [
        green_times.reshape(JUMP, STEPS, NO, NO),
        screened[0],
        bare_green.reshape(JUMP, STEPS, 2, NO, NO),
    ] + tables()
    buffer = lambda *s: pltpu.VMEM(s, BF16)
    floats = lambda *s: pltpu.VMEM(s, F32)
    dma = lambda *s: pltpu.SemaphoreType.DMA(s)
    whole = pl.BlockSpec(memory_space=VMEM)
    mixed = pl.pallas_call(
        kernel,
        out_shape=jax.ShapeDtypeStruct((JUMP, STEPS, NO, NO), BF16),
        in_specs=[whole, whole, pl.BlockSpec(memory_space=pl.ANY)] + [whole] * 8,
        out_specs=whole,
        scratch_shapes=[
            buffer(STEPS, KA, JUMP, SUB, NO),
            buffer(2, STEPS, SUB, 32, NO),
            buffer(SUB, COUNT, NO),
            buffer(STEPS, SUB, 32, NO),
            buffer(STEPS, SUB, 32, NO),
            buffer(STEPS, Z, X, 2, 16, NO),
            buffer(2, STEPS, TAU, 2, 16, NO),
            buffer(STEPS, Y, X * C, 2, 16, NO),
            buffer(2, STEPS, LAYER, 2, 16, NO),
            buffer(STEPS, LAYER, 2, 16, NO),
            buffer(2, STEPS, Y, X * C, 2, 16, NO),
            buffer(STEPS, TAU, 2, 16, NO),
            buffer(2, STEPS, Z, X, 2, 16, NO),
            buffer(STEPS, KA, JUMP, SUB, NO),
            buffer(2, JUMP, STEPS, NO, NO),
            buffer(STEPS, 2, 2, 2, NO, NO),
            floats(3, 8, NO),
            floats(8, 128),
            floats(TAU, 8, 128),
            floats(8, 128),
            floats(KA, 8, 128),
            dma(STEPS, 2),
            dma(STEPS, 2, 2),
            dma(STEPS, JUMP),
            dma(2, STEPS, 2),
            dma(2, STEPS, 2),
            dma(2, STEPS, 2),
            dma(2, STEPS, 2),
            dma(2, STEPS, 2),
            dma(2, 2),
        ],
        compiler_params=pltpu.CompilerParams(
            collective_id=0, has_side_effects=True, vmem_limit_bytes=LIMIT
        ),
    )(*operands)
    return mixed.reshape(green_times.shape)


def solution(mesh):
    return jax.shard_map(
        per_device,
        mesh=mesh,
        in_specs=(
            P("tau", "ka", None, None),
            P("tau", None, "ka", None),
            P("tau", "ka", None, None, None),
        ),
        out_specs=P("tau", "ka", None, None),
        check_vma=False,
    )
```

```python
import math

import jax
import jax.numpy as jnp
import numpy as np
from jax import lax
from jax.experimental import pallas as pl
from jax.experimental.pallas import tpu as pltpu
from jax.sharding import PartitionSpec as P

KX = 6
KY = 4
KZ = 4
TURNS = 2
F32 = jnp.float32
BF16 = jnp.bfloat16
MESH = pl.DeviceIdType.MESH

Z, X, Y, C = 8, 4, 4, 2
TAU = Z * X
KA = Y * C
NO = 256
SUB = NO // KA
STEPS = 3
JUMP = 4
COUNT = KX * KY * KZ
VMEM = pltpu.VMEM
LIMIT = 60 << 20


def hartley_table():
    position = np.arange(COUNT)
    one = position // (KY * KZ)
    two = position // KZ % KY
    three = position % KZ
    phase = (
        one[:, None] * one[None, :] * (KY * KZ)
        + two[:, None] * two[None, :] * (KX * KZ)
        + three[:, None] * three[None, :] * (KX * KY)
    ) % COUNT
    angle = phase * (2.0 * math.pi / COUNT)
    return (np.cos(angle) + np.sin(angle)) / math.sqrt(COUNT)


def time_tables(points):
    odd = 2 * np.arange(points) + 1
    angle = (odd[:, None] * odd[None, :] % (4 * points)) * (math.pi / (2 * points))
    factor = 1.0 / math.sqrt(points)
    return np.stack([np.cos(angle) * factor, np.sin(angle) * factor])


def tables():
    s, z, x = np.meshgrid(np.arange(STEPS), np.arange(Z), np.arange(X), indexing="ij")
    j = z % JUMP
    order = (((x - j - s) % Y * C + z // JUMP) * JUMP + j) * STEPS + s
    lattice = hartley_table()
    to_cells = lattice[:, order.reshape(-1)]
    to_points = lattice[order.reshape(-1), :]
    x, c, i = np.meshgrid(np.arange(X), np.arange(C), np.arange(2), indexing="ij")
    pairs = ((c + 2 * i) * X + x).reshape(-1)
    times = time_tables(TAU)[:, pairs, :]
    to_freq = np.einsum("pmt,uv->mputv", times, np.eye(16)).reshape(512, 512)
    swap = np.eye(256).reshape(16, 16, 256).swapaxes(0, 1).reshape(256, 256)
    arrays = (to_cells, to_points, to_freq, to_freq.T, swap)
    return [jnp.asarray(v, BF16) for v in arrays]


def take(ref, sem):
    pltpu.make_async_copy(ref, ref, sem).wait()


def mul(left, right):
    return jnp.dot(left, right, preferred_element_type=F32)


def turn_over(swap, block):
    return mul(swap[...], block.reshape(256, NO)).astype(BF16).reshape(16, 16, NO)


def block_rows(b):
    return pl.ds(pl.multiple_of(b * SUB, SUB), SUB)


def dyson(bare_real, bare_imag, kernel_real, kernel_imag):
    dressed_real, dressed_imag = bare_real, bare_imag
    for turn in range(TURNS):
        new_real = (
            bare_real.astype(F32) + mul(kernel_real, dressed_real) - mul(kernel_imag, dressed_imag)
        )
        new_imag = (
            bare_imag.astype(F32) + mul(kernel_real, dressed_imag) + mul(kernel_imag, dressed_real)
        )
        dressed_real, dressed_imag = new_real.astype(BF16), new_imag.astype(BF16)
    return new_real, new_imag


def kernel(
    x_home, screened, bare, to_cells, to_points, to_freq, to_time, swap,
    out,
    x_parts, x, w, y, sigma, sigma_out, sigma_in, freq_out, freq_in, dressed_out, dressed_in,
    time_out, time_in, home, bare_in, partial, sums, tau_sums, part_sums, ka_sums,
    x_sems, bare_sems, leave_sems, sigma_sems, freq_sems, dressed_sems, time_sems, home_sems,
    sum_sems,
):
    t, a = lax.axis_index("tau"), lax.axis_index("ka")
    my_z, my_x = t // X, lax.rem(t, X)
    my_y, my_c = a // C, lax.rem(a, C)
    my_j = lax.rem(my_z, JUMP)
    my_rows = block_rows(a)

    def start(src, dst, send_sem, recv_sem, device):
        pltpu.make_async_remote_copy(
            src_ref=src, dst_ref=dst, send_sem=send_sem, recv_sem=recv_sem,
            device_id=device, device_id_type=MESH,
        ).start()

    def send(src, dst, sems, device):
        start(src, dst, sems.at[0], sems.at[1], device)

    def loop(count, body):
        def step(d, c):
            body(d)
            return c

        lax.fori_loop(1, count, step, 0)

    def tau_peer(d):
        turn = lax.rem(d, Z)
        far = jnp.where(lax.rem(turn, 2) == 1, (turn + 1) // 2, Z - turn // 2)
        z, other_x = lax.rem(my_z + far, Z), lax.rem(my_x + d // Z, X)
        return z * X + other_x, (z * X + other_x, a)

    def ka_peer(d):
        b = lax.rem(a + d, KA)
        return b, (t, b)

    low = my_z < Z // 2
    row = jnp.where(low, my_z, Z - 1 - my_z)
    column = jnp.where(low, my_x, X - 1 - my_x)
    goal_i, goal_f = row // 2, jnp.where(low, 0, 1)

    def goal(j, s):
        z, other_x = my_c * JUMP + j, lax.rem(my_y + j + s, X)
        b = lax.rem(column + j + s, Y) * C + lax.rem(row, 2)
        here = (z == my_z) & (other_x == my_x) & (b == a)
        return here, (z * X + other_x, b)

    def own_column(s):
        return lax.rem(my_y + 2 * Y - my_j - s, Y)

    def origin(i, f, s):
        z = my_c + 2 * i if f == 0 else Z - 1 - (my_c + 2 * i)
        other_x = own_column(s) if f == 0 else X - 1 - own_column(s)
        b = lax.rem(my_x + 2 * X - my_j - s, X) * C + my_z // JUMP
        here = (z == my_z) & (other_x == my_x) & (b == a)
        return here, (z * X + other_x, b)

    barrier = pltpu.get_barrier_semaphore()

    def greet(device):
        pl.semaphore_signal(barrier, inc=1, device_id=device, device_id_type=MESH)

    loop(TAU, lambda d: greet(tau_peer(d)[1]))
    loop(KA, lambda d: greet(ka_peer(d)[1]))
    greeters = TAU - 1 + KA - 1
    for s in range(STEPS):
        for i in range(2):
            for f in range(2):
                here, device = origin(i, f, s)
                pl.when(jnp.logical_not(here))(lambda device=device: greet(device))
        for j in range(JUMP):
            greeters += jnp.where(goal(j, s)[0], 0, 1)
    pl.semaphore_wait(barrier, greeters)

    for s in range(STEPS):

        def spread(d):
            b, device = ka_peer(d)
            send(x_home.at[:, s, block_rows(b), :], x_parts.at[s, a], x_sems.at[s], device)

        loop(KA, spread)
        x_parts[s, a] = x_home[:, s, my_rows, :]
    for s in range(STEPS):
        for j in range(JUMP):
            here, device = goal(j, s)
            arrived = bare_sems.at[s, goal_i, goal_f]
            target = bare_in.at[s, goal_i, goal_f]

            @pl.when(jnp.logical_not(here))
            def _():
                start(bare.at[j, s], target, leave_sems.at[s, j], arrived, device)

            @pl.when(here)
            def _():
                pltpu.make_async_copy(bare.at[j, s], target, arrived).start()

    for cells in range(COUNT // 16):
        for uh in range(2):
            rows, columns = pl.ds(uh * 16, 16), pl.ds(cells * 16, 16)
            w[rows, columns, :] = turn_over(swap, screened[columns, rows, :])
    for s in range(STEPS):
        take(x_parts.at[s, pl.ds(0, KA - 1)], x_sems.at[s, 1])
        for c in range(C):
            for uh in range(2):
                rows = pl.ds(uh * 16, 16)
                parts = [(j, (other_x - j - s) % Y) for j in range(JUMP) for other_x in range(X)]
                block = jnp.stack([x_parts[s, b * C + c, j, rows, :] for j, b in parts])
                x[0, s, rows, pl.ds(c * 16, 16), :] = turn_over(swap, block)

    def one_round(turn):
        def lattice(u, c):
            block = x[turn, :, u].reshape(COUNT, NO)
            cells = mul(to_cells[...], block)
            sigma_cells = (-cells * w[u].astype(F32)).astype(BF16)
            sigma[:, u] = mul(to_points[...], sigma_cells).astype(BF16).reshape(STEPS, TAU, NO)
            return c

        lax.fori_loop(0, SUB, lattice, 0, unroll=4)
        if turn:
            for s in range(STEPS):
                take(sigma_in.at[0, s, pl.ds(0, TAU - 1)], sigma_sems.at[0, s, 0])
                take(dressed_in.at[0, s, pl.ds(0, KA - 1)], freq_sems.at[0, s, 0])
                take(dressed_in.at[0, s, pl.ds(0, KA - 1)], dressed_sems.at[0, s, 0])
                take(sigma_in.at[0, s, pl.ds(0, TAU - 1)], time_sems.at[0, s, 0])

        for s in range(STEPS):
            for zh in range(2):
                for uh in range(2):
                    rows, points = pl.ds(uh * 16, 16), pl.ds(zh * 16, 16)
                    sigma_out[s, points, rows, :] = turn_over(swap, sigma[s, rows, points, :])

            def part(d):
                n, device = tau_peer(d)
                send(sigma_out.at[s, n], sigma_in.at[turn, s, t], sigma_sems.at[turn, s], device)

            loop(TAU, part)
            sigma_in[turn, s, t] = sigma_out[s, t]

        def to_frequencies(s):
            take(sigma_in.at[turn, s, pl.ds(0, TAU - 1)], sigma_sems.at[turn, s, 1])
            for uh in range(2):
                rows = pl.ds(uh * 16, 16)
                block = sigma_in[turn, s, :, rows, :].reshape(512, NO)
                value = mul(to_freq[...], block).astype(BF16)
                freq_out[s, :, :, :, rows, :] = value.reshape(KA, 2, 2, 16, NO)

            def place(b):
                return lax.rem(b // C + 2 * Y - my_j - s, Y) * C + lax.rem(b, C)

            def part(d):
                b, device = ka_peer(d)
                send(
                    freq_out.at[s, place(b)], freq_in.at[turn, s, :, :, my_rows, :],
                    freq_sems.at[turn, s], device,
                )

            loop(KA, part)
            freq_in[turn, s, :, :, my_rows, :] = freq_out[s, place(a)]

        def solve(s):
            take(dressed_in.at[turn, s, pl.ds(0, KA - 1)], freq_sems.at[turn, s, 1])
            if turn == 0:
                for i in range(2):
                    for f in range(2):
                        take(bare_in.at[s, i, f], bare_sems.at[s, i, f])

            def one(i, c):
                real, imag = freq_in[turn, s, i, 0], freq_in[turn, s, i, 1]
                br, bi = bare_in[s, i, 0, 0], bare_in[s, i, 0, 1]
                kr = (mul(br, real) - mul(bi, imag)).astype(BF16)
                ki = (mul(br, imag) + mul(bi, real)).astype(BF16)
                low_real, low_imag = dyson(br, bi, kr, ki)
                br, bi = bare_in[s, i, 1, 0], bare_in[s, i, 1, 1]
                kr = (-(mul(br, real) + mul(bi, imag))).astype(BF16)
                ki = (mul(br, imag) - mul(bi, real)).astype(BF16)
                high_real, high_imag = dyson(br, bi, kr, ki)
                dressed_out[s, i, 0] = (low_real - high_real).astype(BF16)
                dressed_out[s, i, 1] = (low_imag + high_imag).astype(BF16)
                return c

            lax.fori_loop(0, 2, one, 0)
            target = dressed_in.at[turn, s, own_column(s) * C + my_c]

            def part(d):
                b, device = ka_peer(d)
                send(
                    dressed_out.at[s, :, :, block_rows(b), :], target,
                    dressed_sems.at[turn, s], device,
                )

            loop(KA, part)
            dressed_in[turn, s, own_column(s) * C + my_c] = dressed_out[s, :, :, my_rows, :]

        def to_times(s):
            take(dressed_in.at[turn, s, pl.ds(0, KA - 1)], dressed_sems.at[turn, s, 1])
            for uh in range(2):
                rows = pl.ds(uh * 16, 16)
                block = dressed_in[turn, s, :, :, :, rows, :].reshape(512, NO)
                value = mul(to_time[...], block).astype(BF16)
                time_out[s, :, rows, :] = value.reshape(TAU, 16, NO)

            def part(d):
                n, device = tau_peer(d)
                send(time_out.at[s, n], time_in.at[turn, s, t], time_sems.at[turn, s], device)

            loop(TAU, part)
            time_in[turn, s, t] = time_out[s, t]

        def finish(s):
            take(sigma_in.at[turn, s, pl.ds(0, TAU - 1)], time_sems.at[turn, s, 1])

            def place(b, j):
                return (lax.rem(b, C) * JUMP + j) * X + lax.rem(b // C + j + s, X)

            def part(d):
                b, device = ka_peer(d)
                for j in range(JUMP):
                    send(
                        time_in.at[turn, s, place(b, j)], home.at[turn, j, s, my_rows, :],
                        home_sems.at[turn, s], device,
                    )

            loop(KA, part)
            for j in range(JUMP):
                home[turn, j, s, my_rows, :] = time_in[turn, s, place(a, j)]
            for zh in range(2):
                for uh in range(2):
                    rows, points = pl.ds(uh * 16, 16), pl.ds(zh * 16, 16)
                    value = turn_over(swap, time_in[turn, s, points, rows, :])
                    old = x[turn, s, rows, points, :].astype(F32)
                    if turn == 0:
                        y[s, rows, points, :] = value
                        x[1, s, rows, points, :] = ((old + value.astype(F32)) * 0.5).astype(BF16)
                    else:
                        begin = x[0, s, rows, points, :].astype(F32)
                        first = y[s, rows, points, :].astype(F32) - begin
                        second = value.astype(F32) - old
                        for j, term in enumerate((first * first, first * second, second * second)):
                            partial[j] += jnp.sum(term.reshape(32, 8, NO), axis=0)

        to_frequencies(0)
        to_frequencies(1)
        solve(0)
        to_frequencies(2)
        to_times(0)
        solve(1)
        to_times(1)
        solve(2)
        to_times(2)
        for s in range(STEPS):
            finish(s)

    partial[...] = jnp.zeros_like(partial)
    one_round(0)
    one_round(1)

    index = lax.broadcasted_iota(jnp.int32, (8, 128), 0)
    tile = jnp.zeros((8, 128), F32)
    for j in range(3):
        line = jnp.sum(partial[j], axis=0, keepdims=True)
        line = line[:, :128] + line[:, 128:]
        tile = jnp.where(index == j, jnp.broadcast_to(line, (8, 128)), tile)
    sums[...] = tile
    loop(TAU, lambda d: send(sums, tau_sums.at[t], sum_sems.at[0], tau_peer(d)[1]))
    tau_sums[t] = tile
    take(tau_sums.at[pl.ds(0, TAU - 1)], sum_sems.at[0, 1])
    part_sums[...] = jnp.sum(tau_sums[...], axis=0)
    loop(KA, lambda d: send(part_sums, ka_sums.at[a], sum_sems.at[1], ka_peer(d)[1]))
    ka_sums[a] = part_sums[...]
    take(ka_sums.at[pl.ds(0, KA - 1)], sum_sems.at[1, 1])
    whole = jnp.sum(ka_sums[...], axis=0)
    means = [
        jnp.sum(jnp.where(index == j, whole, 0.0)) * (1.0 / (TAU * COUNT * NO * NO))
        for j in range(3)
    ]
    top = jnp.full((NO, NO), means[2] - means[1], F32)
    weight = top / (means[0] - 2.0 * means[1] + means[2] + 1e-06)
    rest = 1.0 - weight
    for s in range(STEPS):
        for turn in range(2):
            take(x_parts.at[s, pl.ds(0, KA - 1)], home_sems.at[turn, s, 1])
        for j in range(JUMP):
            value = weight * home[0, j, s].astype(F32) + rest * home[1, j, s].astype(F32)
            out[j, s] = value.astype(BF16)

    for s in range(STEPS):
        take(x_parts.at[s, pl.ds(0, KA - 1)], x_sems.at[s, 0])
        take(sigma_in.at[1, s, pl.ds(0, TAU - 1)], sigma_sems.at[1, s, 0])
        take(dressed_in.at[1, s, pl.ds(0, KA - 1)], freq_sems.at[1, s, 0])
        take(dressed_in.at[1, s, pl.ds(0, KA - 1)], dressed_sems.at[1, s, 0])
        take(sigma_in.at[1, s, pl.ds(0, TAU - 1)], time_sems.at[1, s, 0])
        for turn in range(2):
            take(x_parts.at[s, pl.ds(0, KA - 1)], home_sems.at[turn, s, 0])
        for j in range(JUMP):

            @pl.when(jnp.logical_not(goal(j, s)[0]))
            def _():
                take(bare.at[j, s], leave_sems.at[s, j])

    take(tau_sums.at[pl.ds(0, TAU - 1)], sum_sems.at[0, 0])
    take(ka_sums.at[pl.ds(0, KA - 1)], sum_sems.at[1, 0])


def per_device(green_times, screened, bare_green):
    operands = [
        green_times.reshape(JUMP, STEPS, NO, NO),
        screened[0],
        bare_green.reshape(JUMP, STEPS, 2, NO, NO),
    ] + tables()
    buffer = lambda *s: pltpu.VMEM(s, BF16)
    floats = lambda *s: pltpu.VMEM(s, F32)
    dma = lambda *s: pltpu.SemaphoreType.DMA(s)
    whole = pl.BlockSpec(memory_space=VMEM)
    mixed = pl.pallas_call(
        kernel,
        out_shape=jax.ShapeDtypeStruct((JUMP, STEPS, NO, NO), BF16),
        in_specs=[whole, whole, pl.BlockSpec(memory_space=pl.ANY)] + [whole] * 5,
        out_specs=whole,
        scratch_shapes=[
            buffer(STEPS, KA, JUMP, SUB, NO),
            buffer(2, STEPS, SUB, TAU, NO),
            buffer(SUB, COUNT, NO),
            buffer(STEPS, SUB, TAU, NO),
            buffer(STEPS, SUB, TAU, NO),
            buffer(STEPS, TAU, SUB, NO),
            buffer(2, STEPS, TAU, SUB, NO),
            buffer(STEPS, KA, 2, 2, SUB, NO),
            buffer(2, STEPS, 2, 2, NO, NO),
            buffer(STEPS, 2, 2, NO, NO),
            buffer(2, STEPS, KA, 2, 2, SUB, NO),
            buffer(STEPS, TAU, SUB, NO),
            buffer(2, STEPS, TAU, SUB, NO),
            buffer(2, JUMP, STEPS, NO, NO),
            buffer(STEPS, 2, 2, 2, NO, NO),
            floats(3, 8, NO),
            floats(8, 128),
            floats(TAU, 8, 128),
            floats(8, 128),
            floats(KA, 8, 128),
            dma(STEPS, 2),
            dma(STEPS, 2, 2),
            dma(STEPS, JUMP),
            dma(2, STEPS, 2),
            dma(2, STEPS, 2),
            dma(2, STEPS, 2),
            dma(2, STEPS, 2),
            dma(2, STEPS, 2),
            dma(2, 2),
        ],
        compiler_params=pltpu.CompilerParams(
            collective_id=0, has_side_effects=True, vmem_limit_bytes=LIMIT
        ),
    )(*operands)
    return mixed.reshape(green_times.shape)


def solution(mesh):
    return jax.shard_map(
        per_device,
        mesh=mesh,
        in_specs=(
            P("tau", "ka", None, None),
            P("tau", None, "ka", None),
            P("tau", "ka", None, None, None),
        ),
        out_specs=P("tau", "ka", None, None),
        check_vma=False,
    )
```

```python
import math

import jax
import jax.numpy as jnp
import numpy as np
from jax import lax
from jax.experimental import pallas as pl
from jax.experimental.pallas import tpu as pltpu
from jax.sharding import PartitionSpec as P

KX = 6
KY = 4
KZ = 4
TURNS = 2
F32 = jnp.float32
BF16 = jnp.bfloat16
MESH = pl.DeviceIdType.MESH

Z, X, Y, C = 8, 4, 4, 2
TAU = Z * X
KA = Y * C
NO = 256
SUB = NO // KA
STEPS = 3
JUMP = 4
COUNT = KX * KY * KZ
VMEM = pltpu.VMEM
LIMIT = 60 << 20


def hartley_table():
    position = np.arange(COUNT)
    one = position // (KY * KZ)
    two = position // KZ % KY
    three = position % KZ
    phase = (
        one[:, None] * one[None, :] * (KY * KZ)
        + two[:, None] * two[None, :] * (KX * KZ)
        + three[:, None] * three[None, :] * (KX * KY)
    ) % COUNT
    angle = phase * (2.0 * math.pi / COUNT)
    return (np.cos(angle) + np.sin(angle)) / math.sqrt(COUNT)


def time_tables(points):
    odd = 2 * np.arange(points) + 1
    angle = (odd[:, None] * odd[None, :] % (4 * points)) * (math.pi / (2 * points))
    factor = 1.0 / math.sqrt(points)
    return np.stack([np.cos(angle) * factor, np.sin(angle) * factor])


def tables():
    s, z, x = np.meshgrid(np.arange(STEPS), np.arange(Z), np.arange(X), indexing="ij")
    j = z % JUMP
    order = (((x - j - s) % Y * C + z // JUMP) * JUMP + j) * STEPS + s
    lattice = hartley_table()
    to_cells = lattice[:, order.reshape(-1)]
    to_points = lattice[order.reshape(-1), :]
    x, c, i = np.meshgrid(np.arange(X), np.arange(C), np.arange(2), indexing="ij")
    pairs = ((c + 2 * i) * X + x).reshape(-1)
    times = time_tables(TAU)[:, pairs, :]
    to_freq = np.einsum("pmt,uv->mputv", times, np.eye(16)).reshape(512, 512)
    swap = np.eye(256).reshape(16, 16, 256).swapaxes(0, 1).reshape(256, 256)
    arrays = (to_cells, to_points, to_freq, to_freq.T, swap)
    return [jnp.asarray(v, BF16) for v in arrays]


def take(ref, sem):
    pltpu.make_async_copy(ref, ref, sem).wait()


def mul(left, right):
    return jnp.dot(left, right, preferred_element_type=F32)


def turn_over(swap, block):
    return mul(swap[...], block.reshape(256, NO)).astype(BF16).reshape(16, 16, NO)


def block_rows(b):
    return pl.ds(pl.multiple_of(b * SUB, SUB), SUB)


def dyson(bare_real, bare_imag, kernel_real, kernel_imag):
    dressed_real, dressed_imag = bare_real, bare_imag
    for turn in range(TURNS):
        new_real = (
            bare_real.astype(F32) + mul(kernel_real, dressed_real) - mul(kernel_imag, dressed_imag)
        )
        new_imag = (
            bare_imag.astype(F32) + mul(kernel_real, dressed_imag) + mul(kernel_imag, dressed_real)
        )
        dressed_real, dressed_imag = new_real.astype(BF16), new_imag.astype(BF16)
    return new_real, new_imag


def kernel(
    x_home, screened, bare, to_cells, to_points, to_freq, to_time, swap,
    out,
    x_parts, x, w, y, sigma, sigma_out, sigma_in, freq_out, freq_in, dressed_out, dressed_in,
    time_out, time_in, home, bare_in, partial, sums, tau_sums, part_sums, ka_sums,
    x_sems, bare_sems, leave_sems, sigma_sems, freq_sems, dressed_sems, time_sems, home_sems,
    sum_sems,
):
    t, a = lax.axis_index("tau"), lax.axis_index("ka")
    my_z, my_x = t // X, lax.rem(t, X)
    my_y, my_c = a // C, lax.rem(a, C)
    my_j = lax.rem(my_z, JUMP)
    my_rows = block_rows(a)

    def start(src, dst, send_sem, recv_sem, device):
        pltpu.make_async_remote_copy(
            src_ref=src, dst_ref=dst, send_sem=send_sem, recv_sem=recv_sem,
            device_id=device, device_id_type=MESH,
        ).start()

    def send(src, dst, sems, device):
        start(src, dst, sems.at[0], sems.at[1], device)

    def loop(count, body):
        def step(d, c):
            body(d)
            return c

        lax.fori_loop(1, count, step, 0)

    def tau_peer(d):
        turn = lax.rem(d, Z)
        far = jnp.where(lax.rem(turn, 2) == 1, (turn + 1) // 2, Z - turn // 2)
        z, other_x = lax.rem(my_z + far, Z), lax.rem(my_x + d // Z, X)
        return z * X + other_x, (z * X + other_x, a)

    def ka_peer(d):
        b = lax.rem(a + d, KA)
        return b, (t, b)

    low = my_z < Z // 2
    row = jnp.where(low, my_z, Z - 1 - my_z)
    column = jnp.where(low, my_x, X - 1 - my_x)
    goal_i, goal_f = row // 2, jnp.where(low, 0, 1)

    def goal(j, s):
        z, other_x = my_c * JUMP + j, lax.rem(my_y + j + s, X)
        b = lax.rem(column + j + s, Y) * C + lax.rem(row, 2)
        here = (z == my_z) & (other_x == my_x) & (b == a)
        return here, (z * X + other_x, b)

    def own_column(s):
        return lax.rem(my_y + 2 * Y - my_j - s, Y)

    def origin(i, f, s):
        z = my_c + 2 * i if f == 0 else Z - 1 - (my_c + 2 * i)
        other_x = own_column(s) if f == 0 else X - 1 - own_column(s)
        b = lax.rem(my_x + 2 * X - my_j - s, X) * C + my_z // JUMP
        here = (z == my_z) & (other_x == my_x) & (b == a)
        return here, (z * X + other_x, b)

    barrier = pltpu.get_barrier_semaphore()

    def greet(device):
        pl.semaphore_signal(barrier, inc=1, device_id=device, device_id_type=MESH)

    loop(TAU, lambda d: greet(tau_peer(d)[1]))
    loop(KA, lambda d: greet(ka_peer(d)[1]))
    greeters = TAU - 1 + KA - 1
    for s in range(STEPS):
        for i in range(2):
            for f in range(2):
                here, device = origin(i, f, s)
                pl.when(jnp.logical_not(here))(lambda device=device: greet(device))
        for j in range(JUMP):
            greeters += jnp.where(goal(j, s)[0], 0, 1)
    pl.semaphore_wait(barrier, greeters)

    for s in range(STEPS):

        def spread(d):
            b, device = ka_peer(d)
            send(x_home.at[:, s, block_rows(b), :], x_parts.at[s, a], x_sems.at[s], device)

        loop(KA, spread)
        x_parts[s, a] = x_home[:, s, my_rows, :]
    for s in range(STEPS):
        for j in range(JUMP):
            here, device = goal(j, s)
            arrived = bare_sems.at[s, goal_i, goal_f]
            target = bare_in.at[s, goal_i, goal_f]

            @pl.when(jnp.logical_not(here))
            def _():
                start(bare.at[j, s], target, leave_sems.at[s, j], arrived, device)

            @pl.when(here)
            def _():
                pltpu.make_async_copy(bare.at[j, s], target, arrived).start()

    for cells in range(COUNT // 16):
        for uh in range(2):
            rows, columns = pl.ds(uh * 16, 16), pl.ds(cells * 16, 16)
            w[rows, columns, :] = turn_over(swap, screened[columns, rows, :])
    for s in range(STEPS):
        take(x_parts.at[s, pl.ds(0, KA - 1)], x_sems.at[s, 1])
        for c in range(C):
            for uh in range(2):
                rows = pl.ds(uh * 16, 16)
                parts = [(j, (other_x - j - s) % Y) for j in range(JUMP) for other_x in range(X)]
                block = jnp.stack([x_parts[s, b * C + c, j, rows, :] for j, b in parts])
                x[0, s, rows, pl.ds(c * 16, 16), :] = turn_over(swap, block)

    def one_round(turn):
        def lattice(u, c):
            block = x[turn, :, u].reshape(COUNT, NO)
            cells = mul(to_cells[...], block)
            sigma_cells = (-cells * w[u].astype(F32)).astype(BF16)
            sigma[:, u] = mul(to_points[...], sigma_cells).astype(BF16).reshape(STEPS, TAU, NO)
            return c

        lax.fori_loop(0, SUB, lattice, 0, unroll=4)
        if turn:
            for s in range(STEPS):
                for uh in range(2):
                    take(sigma_in.at[0, s, uh, pl.ds(0, TAU - 1)], sigma_sems.at[0, s, uh, 0])
                take(dressed_in.at[0, s, pl.ds(0, KA - 1)], freq_sems.at[0, s, 0])
                take(dressed_in.at[0, s, pl.ds(0, KA - 1)], dressed_sems.at[0, s, 0])
                take(time_in.at[0, s, pl.ds(0, TAU - 1)], time_sems.at[0, s, 0])

        for s in range(STEPS):
            for zh in range(2):
                for uh in range(2):
                    rows, points = pl.ds(uh * 16, 16), pl.ds(zh * 16, 16)
                    sigma_out[s, uh, points] = turn_over(swap, sigma[s, rows, points, :])
            for uh in range(2):

                def part(d):
                    n, device = tau_peer(d)
                    send(
                        sigma_out.at[s, uh, n], sigma_in.at[turn, s, uh, t],
                        sigma_sems.at[turn, s, uh], device,
                    )

                loop(TAU, part)
                sigma_in[turn, s, uh, t] = sigma_out[s, uh, t]

        def to_frequencies(s):
            def place(b):
                return lax.rem(b // C + 2 * Y - my_j - s, Y) * C + lax.rem(b, C)

            for uh in range(2):
                take(sigma_in.at[turn, s, uh, pl.ds(0, TAU - 1)], sigma_sems.at[turn, s, uh, 1])
                block = sigma_in[turn, s, uh].reshape(512, NO)
                value = mul(to_freq[...], block).astype(BF16)
                freq_out[s, uh] = value.reshape(KA, 2, 2, 16, NO)
                rows = pl.ds(pl.multiple_of(a * SUB + uh * 16, 16), 16)

                def part(d):
                    b, device = ka_peer(d)
                    send(
                        freq_out.at[s, uh, place(b)], freq_in.at[turn, s, :, :, rows, :],
                        freq_sems.at[turn, s], device,
                    )

                loop(KA, part)
                freq_in[turn, s, :, :, rows, :] = freq_out[s, uh, place(a)]

        def solve(s):
            take(dressed_in.at[turn, s, pl.ds(0, KA - 1)], freq_sems.at[turn, s, 1])
            if turn == 0:
                for i in range(2):
                    for f in range(2):
                        take(bare_in.at[s, i, f], bare_sems.at[s, i, f])

            def one(i, c):
                real, imag = freq_in[turn, s, i, 0], freq_in[turn, s, i, 1]
                br, bi = bare_in[s, i, 0, 0], bare_in[s, i, 0, 1]
                kr = (mul(br, real) - mul(bi, imag)).astype(BF16)
                ki = (mul(br, imag) + mul(bi, real)).astype(BF16)
                low_real, low_imag = dyson(br, bi, kr, ki)
                br, bi = bare_in[s, i, 1, 0], bare_in[s, i, 1, 1]
                kr = (-(mul(br, real) + mul(bi, imag))).astype(BF16)
                ki = (mul(br, imag) - mul(bi, real)).astype(BF16)
                high_real, high_imag = dyson(br, bi, kr, ki)
                dressed_out[s, i, 0] = (low_real - high_real).astype(BF16)
                dressed_out[s, i, 1] = (low_imag + high_imag).astype(BF16)
                return c

            lax.fori_loop(0, 2, one, 0)
            target = dressed_in.at[turn, s, own_column(s) * C + my_c]

            def part(d):
                b, device = ka_peer(d)
                send(
                    dressed_out.at[s, :, :, block_rows(b), :], target,
                    dressed_sems.at[turn, s], device,
                )

            loop(KA, part)
            dressed_in[turn, s, own_column(s) * C + my_c] = dressed_out[s, :, :, my_rows, :]

        def to_times(s):
            take(dressed_in.at[turn, s, pl.ds(0, KA - 1)], dressed_sems.at[turn, s, 1])
            for uh in range(2):
                rows = pl.ds(uh * 16, 16)
                block = dressed_in[turn, s, :, :, :, rows, :].reshape(512, NO)
                value = mul(to_time[...], block).astype(BF16)
                time_out[s, :, rows, :] = value.reshape(TAU, 16, NO)

            def part(d):
                n, device = tau_peer(d)
                send(time_out.at[s, n], time_in.at[turn, s, t], time_sems.at[turn, s], device)

            loop(TAU, part)
            time_in[turn, s, t] = time_out[s, t]

        def finish(s):
            take(time_in.at[turn, s, pl.ds(0, TAU - 1)], time_sems.at[turn, s, 1])

            def place(b, j):
                return (lax.rem(b, C) * JUMP + j) * X + lax.rem(b // C + j + s, X)

            def part(d):
                b, device = ka_peer(d)
                for j in range(JUMP):
                    send(
                        time_in.at[turn, s, place(b, j)], home.at[turn, j, s, my_rows, :],
                        home_sems.at[turn, s], device,
                    )

            loop(KA, part)
            for j in range(JUMP):
                home[turn, j, s, my_rows, :] = time_in[turn, s, place(a, j)]
            for zh in range(2):
                for uh in range(2):
                    rows, points = pl.ds(uh * 16, 16), pl.ds(zh * 16, 16)
                    value = turn_over(swap, time_in[turn, s, points, rows, :])
                    old = x[turn, s, rows, points, :].astype(F32)
                    if turn == 0:
                        y[s, rows, points, :] = value
                        x[1, s, rows, points, :] = ((old + value.astype(F32)) * 0.5).astype(BF16)
                    else:
                        begin = x[0, s, rows, points, :].astype(F32)
                        first = y[s, rows, points, :].astype(F32) - begin
                        second = value.astype(F32) - old
                        for j, term in enumerate((first * first, first * second, second * second)):
                            partial[j] += jnp.sum(term.reshape(32, 8, NO), axis=0)

        to_frequencies(0)
        to_frequencies(1)
        solve(0)
        to_frequencies(2)
        to_times(0)
        solve(1)
        to_times(1)
        solve(2)
        to_times(2)
        for s in range(STEPS):
            finish(s)

    partial[...] = jnp.zeros_like(partial)
    one_round(0)
    one_round(1)

    index = lax.broadcasted_iota(jnp.int32, (8, 128), 0)
    tile = jnp.zeros((8, 128), F32)
    for j in range(3):
        line = jnp.sum(partial[j], axis=0, keepdims=True)
        line = line[:, :128] + line[:, 128:]
        tile = jnp.where(index == j, jnp.broadcast_to(line, (8, 128)), tile)
    sums[...] = tile
    loop(TAU, lambda d: send(sums, tau_sums.at[t], sum_sems.at[0], tau_peer(d)[1]))
    tau_sums[t] = tile
    take(tau_sums.at[pl.ds(0, TAU - 1)], sum_sems.at[0, 1])
    part_sums[...] = jnp.sum(tau_sums[...], axis=0)
    loop(KA, lambda d: send(part_sums, ka_sums.at[a], sum_sems.at[1], ka_peer(d)[1]))
    ka_sums[a] = part_sums[...]
    take(ka_sums.at[pl.ds(0, KA - 1)], sum_sems.at[1, 1])
    whole = jnp.sum(ka_sums[...], axis=0)
    means = [
        jnp.sum(jnp.where(index == j, whole, 0.0)) * (1.0 / (TAU * COUNT * NO * NO))
        for j in range(3)
    ]
    top = jnp.full((NO, NO), means[2] - means[1], F32)
    weight = top / (means[0] - 2.0 * means[1] + means[2] + 1e-06)
    rest = 1.0 - weight
    for s in range(STEPS):
        for turn in range(2):
            take(x_parts.at[s, pl.ds(0, KA - 1)], home_sems.at[turn, s, 1])
        for j in range(JUMP):
            value = weight * home[0, j, s].astype(F32) + rest * home[1, j, s].astype(F32)
            out[j, s] = value.astype(BF16)

    for s in range(STEPS):
        take(x_parts.at[s, pl.ds(0, KA - 1)], x_sems.at[s, 0])
        for uh in range(2):
            take(sigma_in.at[1, s, uh, pl.ds(0, TAU - 1)], sigma_sems.at[1, s, uh, 0])
        take(dressed_in.at[1, s, pl.ds(0, KA - 1)], freq_sems.at[1, s, 0])
        take(dressed_in.at[1, s, pl.ds(0, KA - 1)], dressed_sems.at[1, s, 0])
        take(time_in.at[1, s, pl.ds(0, TAU - 1)], time_sems.at[1, s, 0])
        for turn in range(2):
            take(x_parts.at[s, pl.ds(0, KA - 1)], home_sems.at[turn, s, 0])
        for j in range(JUMP):

            @pl.when(jnp.logical_not(goal(j, s)[0]))
            def _():
                take(bare.at[j, s], leave_sems.at[s, j])

    take(tau_sums.at[pl.ds(0, TAU - 1)], sum_sems.at[0, 0])
    take(ka_sums.at[pl.ds(0, KA - 1)], sum_sems.at[1, 0])


def per_device(green_times, screened, bare_green):
    operands = [
        green_times.reshape(JUMP, STEPS, NO, NO),
        screened[0],
        bare_green.reshape(JUMP, STEPS, 2, NO, NO),
    ] + tables()
    buffer = lambda *s: pltpu.VMEM(s, BF16)
    floats = lambda *s: pltpu.VMEM(s, F32)
    dma = lambda *s: pltpu.SemaphoreType.DMA(s)
    whole = pl.BlockSpec(memory_space=VMEM)
    mixed = pl.pallas_call(
        kernel,
        out_shape=jax.ShapeDtypeStruct((JUMP, STEPS, NO, NO), BF16),
        in_specs=[whole, whole, pl.BlockSpec(memory_space=pl.ANY)] + [whole] * 5,
        out_specs=whole,
        scratch_shapes=[
            buffer(STEPS, KA, JUMP, SUB, NO),
            buffer(2, STEPS, SUB, TAU, NO),
            buffer(SUB, COUNT, NO),
            buffer(STEPS, SUB, TAU, NO),
            buffer(STEPS, SUB, TAU, NO),
            buffer(STEPS, 2, TAU, 16, NO),
            buffer(2, STEPS, 2, TAU, 16, NO),
            buffer(STEPS, 2, KA, 2, 2, 16, NO),
            buffer(2, STEPS, 2, 2, NO, NO),
            buffer(STEPS, 2, 2, NO, NO),
            buffer(2, STEPS, KA, 2, 2, SUB, NO),
            buffer(STEPS, TAU, SUB, NO),
            buffer(2, STEPS, TAU, SUB, NO),
            buffer(2, JUMP, STEPS, NO, NO),
            buffer(STEPS, 2, 2, 2, NO, NO),
            floats(3, 8, NO),
            floats(8, 128),
            floats(TAU, 8, 128),
            floats(8, 128),
            floats(KA, 8, 128),
            dma(STEPS, 2),
            dma(STEPS, 2, 2),
            dma(STEPS, JUMP),
            dma(2, STEPS, 2, 2),
            dma(2, STEPS, 2),
            dma(2, STEPS, 2),
            dma(2, STEPS, 2),
            dma(2, STEPS, 2),
            dma(2, 2),
        ],
        compiler_params=pltpu.CompilerParams(
            collective_id=0, has_side_effects=True, vmem_limit_bytes=LIMIT
        ),
    )(*operands)
    return mixed.reshape(green_times.shape)


def solution(mesh):
    return jax.shard_map(
        per_device,
        mesh=mesh,
        in_specs=(
            P("tau", "ka", None, None),
            P("tau", None, "ka", None),
            P("tau", "ka", None, None, None),
        ),
        out_specs=P("tau", "ka", None, None),
        check_vma=False,
    )
```

```python
import math

import jax
import jax.numpy as jnp
import numpy as np
from jax import lax
from jax.experimental import pallas as pl
from jax.experimental.pallas import tpu as pltpu
from jax.sharding import PartitionSpec as P

KX = 6
KY = 4
KZ = 4
TURNS = 2
F32 = jnp.float32
BF16 = jnp.bfloat16
MESH = pl.DeviceIdType.MESH

Z, X, Y, C = 8, 4, 4, 2
TAU = Z * X
KA = Y * C
NO = 256
SUB = NO // KA
STEPS = 3
JUMP = 4
COUNT = KX * KY * KZ
VMEM = pltpu.VMEM
LIMIT = 60 << 20


def hartley_table():
    position = np.arange(COUNT)
    one = position // (KY * KZ)
    two = position // KZ % KY
    three = position % KZ
    phase = (
        one[:, None] * one[None, :] * (KY * KZ)
        + two[:, None] * two[None, :] * (KX * KZ)
        + three[:, None] * three[None, :] * (KX * KY)
    ) % COUNT
    angle = phase * (2.0 * math.pi / COUNT)
    return (np.cos(angle) + np.sin(angle)) / math.sqrt(COUNT)


def time_tables(points):
    odd = 2 * np.arange(points) + 1
    angle = (odd[:, None] * odd[None, :] % (4 * points)) * (math.pi / (2 * points))
    factor = 1.0 / math.sqrt(points)
    return np.stack([np.cos(angle) * factor, np.sin(angle) * factor])


def tables():
    s, z, x = np.meshgrid(np.arange(STEPS), np.arange(Z), np.arange(X), indexing="ij")
    j = z % JUMP
    order = (((x - j - s) % Y * C + z // JUMP) * JUMP + j) * STEPS + s
    lattice = hartley_table()
    to_cells = lattice[:, order.reshape(-1)]
    to_points = lattice[order.reshape(-1), :]
    x, c, i = np.meshgrid(np.arange(X), np.arange(C), np.arange(2), indexing="ij")
    pairs = ((c + 2 * i) * X + x).reshape(-1)
    times = time_tables(TAU)[:, pairs, :]
    to_freq = np.einsum("pmt,uv->mputv", times, np.eye(16)).reshape(512, 512)
    swap = np.eye(256).reshape(16, 16, 256).swapaxes(0, 1).reshape(256, 256)
    arrays = (to_cells, to_points, to_freq, to_freq.T, swap)
    return [jnp.asarray(v, BF16) for v in arrays]


def take(ref, sem):
    pltpu.make_async_copy(ref, ref, sem).wait()


def mul(left, right):
    return jnp.dot(left, right, preferred_element_type=F32)


def turn_over(swap, block):
    return mul(swap[...], block.reshape(256, NO)).astype(BF16).reshape(16, 16, NO)


def block_rows(b):
    return pl.ds(pl.multiple_of(b * SUB, SUB), SUB)


def dyson(bare_real, bare_imag, kernel_real, kernel_imag):
    dressed_real, dressed_imag = bare_real, bare_imag
    for turn in range(TURNS):
        new_real = (
            bare_real.astype(F32) + mul(kernel_real, dressed_real) - mul(kernel_imag, dressed_imag)
        )
        new_imag = (
            bare_imag.astype(F32) + mul(kernel_real, dressed_imag) + mul(kernel_imag, dressed_real)
        )
        dressed_real, dressed_imag = new_real.astype(BF16), new_imag.astype(BF16)
    return new_real, new_imag


def kernel(
    x_home, screened, bare, to_cells, to_points, to_freq, to_time, swap,
    out,
    x_parts, x, w, y, sigma, sigma_out, sigma_in, freq_out, freq_in, dressed_out, dressed_in,
    time_out, time_in, home, bare_in, partial, sums, tau_sums, part_sums, ka_sums,
    x_sems, bare_sems, leave_sems, sigma_sems, freq_sems, dressed_sems, time_sems, home_sems,
    sum_sems,
):
    t, a = lax.axis_index("tau"), lax.axis_index("ka")
    my_z, my_x = t // X, lax.rem(t, X)
    my_y, my_c = a // C, lax.rem(a, C)
    my_j = lax.rem(my_z, JUMP)
    my_rows = block_rows(a)

    def start(src, dst, send_sem, recv_sem, device):
        pltpu.make_async_remote_copy(
            src_ref=src, dst_ref=dst, send_sem=send_sem, recv_sem=recv_sem,
            device_id=device, device_id_type=MESH,
        ).start()

    def send(src, dst, sems, device):
        start(src, dst, sems.at[0], sems.at[1], device)

    def loop(count, body):
        def step(d, c):
            body(d)
            return c

        lax.fori_loop(1, count, step, 0)

    def tau_peer(d):
        turn = lax.rem(d, Z)
        far = jnp.where(lax.rem(turn, 2) == 1, (turn + 1) // 2, Z - turn // 2)
        z, other_x = lax.rem(my_z + far, Z), lax.rem(my_x + d // Z, X)
        return z * X + other_x, (z * X + other_x, a)

    def ka_peer(d):
        b = lax.rem(a + d, KA)
        return b, (t, b)

    low = my_z < Z // 2
    row = jnp.where(low, my_z, Z - 1 - my_z)
    column = jnp.where(low, my_x, X - 1 - my_x)
    goal_i, goal_f = row // 2, jnp.where(low, 0, 1)

    def goal(j, s):
        z, other_x = my_c * JUMP + j, lax.rem(my_y + j + s, X)
        b = lax.rem(column + j + s, Y) * C + lax.rem(row, 2)
        here = (z == my_z) & (other_x == my_x) & (b == a)
        return here, (z * X + other_x, b)

    def own_column(s):
        return lax.rem(my_y + 2 * Y - my_j - s, Y)

    def origin(i, f, s):
        z = my_c + 2 * i if f == 0 else Z - 1 - (my_c + 2 * i)
        other_x = own_column(s) if f == 0 else X - 1 - own_column(s)
        b = lax.rem(my_x + 2 * X - my_j - s, X) * C + my_z // JUMP
        here = (z == my_z) & (other_x == my_x) & (b == a)
        return here, (z * X + other_x, b)

    barrier = pltpu.get_barrier_semaphore()

    def greet(device):
        pl.semaphore_signal(barrier, inc=1, device_id=device, device_id_type=MESH)

    loop(TAU, lambda d: greet(tau_peer(d)[1]))
    loop(KA, lambda d: greet(ka_peer(d)[1]))
    greeters = TAU - 1 + KA - 1
    for s in range(STEPS):
        for i in range(2):
            for f in range(2):
                here, device = origin(i, f, s)
                pl.when(jnp.logical_not(here))(lambda device=device: greet(device))
        for j in range(JUMP):
            greeters += jnp.where(goal(j, s)[0], 0, 1)
    pl.semaphore_wait(barrier, greeters)

    for s in range(STEPS):

        def spread(d):
            b, device = ka_peer(d)
            send(x_home.at[:, s, block_rows(b), :], x_parts.at[s, a], x_sems.at[s], device)

        loop(KA, spread)
        x_parts[s, a] = x_home[:, s, my_rows, :]
    for s in range(STEPS):
        for j in range(JUMP):
            here, device = goal(j, s)
            arrived = bare_sems.at[s, goal_i, goal_f]
            target = bare_in.at[s, goal_i, goal_f]

            @pl.when(jnp.logical_not(here))
            def _():
                start(bare.at[j, s], target, leave_sems.at[s, j], arrived, device)

            @pl.when(here)
            def _():
                pltpu.make_async_copy(bare.at[j, s], target, arrived).start()

    for cells in range(COUNT // 16):
        for uh in range(2):
            rows, columns = pl.ds(uh * 16, 16), pl.ds(cells * 16, 16)
            w[rows, columns, :] = turn_over(swap, screened[columns, rows, :])
    for s in range(STEPS):
        take(x_parts.at[s, pl.ds(0, KA - 1)], x_sems.at[s, 1])
        for c in range(C):
            for uh in range(2):
                rows = pl.ds(uh * 16, 16)
                parts = [(j, (other_x - j - s) % Y) for j in range(JUMP) for other_x in range(X)]
                block = jnp.stack([x_parts[s, b * C + c, j, rows, :] for j, b in parts])
                x[0, s, rows, pl.ds(c * 16, 16), :] = turn_over(swap, block)

    def one_round(turn):
        def lattice(u, c):
            block = x[turn, :, u].reshape(COUNT, NO)
            cells = mul(to_cells[...], block)
            sigma_cells = (-cells * w[u].astype(F32)).astype(BF16)
            sigma[:, u] = mul(to_points[...], sigma_cells).astype(BF16).reshape(STEPS, TAU, NO)
            return c

        lax.fori_loop(0, SUB, lattice, 0, unroll=4)
        if turn:
            for s in range(STEPS):
                for uh in range(2):
                    take(sigma_in.at[0, s, uh, pl.ds(0, TAU - 1)], sigma_sems.at[0, s, uh, 0])
                take(dressed_in.at[0, s, pl.ds(0, KA - 1)], freq_sems.at[0, s, 0])
                take(dressed_in.at[0, s, pl.ds(0, KA - 1)], dressed_sems.at[0, s, 0])
                take(time_in.at[0, s, pl.ds(0, TAU - 1)], time_sems.at[0, s, 0])

        for s in range(STEPS):
            for zh in range(2):
                for uh in range(2):
                    rows, points = pl.ds(uh * 16, 16), pl.ds(zh * 16, 16)
                    sigma_out[s, uh, points] = turn_over(swap, sigma[s, rows, points, :])
            for uh in range(2):

                def part(d):
                    n, device = tau_peer(d)
                    send(
                        sigma_out.at[s, uh, n], sigma_in.at[turn, s, uh, t],
                        sigma_sems.at[turn, s, uh], device,
                    )

                loop(TAU, part)
                sigma_in[turn, s, uh, t] = sigma_out[s, uh, t]

        def to_frequencies(s):
            def place(b):
                return lax.rem(b // C + 2 * Y - my_j - s, Y) * C + lax.rem(b, C)

            for uh in range(2):
                take(sigma_in.at[turn, s, uh, pl.ds(0, TAU - 1)], sigma_sems.at[turn, s, uh, 1])
                block = sigma_in[turn, s, uh].reshape(512, NO)
                value = mul(to_freq[...], block).astype(BF16)
                freq_out[s, uh] = value.reshape(KA, 2, 2, 16, NO)
                rows = pl.ds(pl.multiple_of(a * SUB + uh * 16, 16), 16)

                def part(d):
                    b, device = ka_peer(d)
                    send(
                        freq_out.at[s, uh, place(b)], freq_in.at[turn, s, :, :, rows, :],
                        freq_sems.at[turn, s], device,
                    )

                loop(KA, part)
                freq_in[turn, s, :, :, rows, :] = freq_out[s, uh, place(a)]

        def solve(s):
            take(dressed_in.at[turn, s, pl.ds(0, KA - 1)], freq_sems.at[turn, s, 1])
            if turn == 0:
                for i in range(2):
                    for f in range(2):
                        take(bare_in.at[s, i, f], bare_sems.at[s, i, f])

            def one(i, c):
                real, imag = freq_in[turn, s, i, 0], freq_in[turn, s, i, 1]
                br, bi = bare_in[s, i, 0, 0], bare_in[s, i, 0, 1]
                kr = (mul(br, real) - mul(bi, imag)).astype(BF16)
                ki = (mul(br, imag) + mul(bi, real)).astype(BF16)
                low_real, low_imag = dyson(br, bi, kr, ki)
                br, bi = bare_in[s, i, 1, 0], bare_in[s, i, 1, 1]
                kr = (-(mul(br, real) + mul(bi, imag))).astype(BF16)
                ki = (mul(br, imag) - mul(bi, real)).astype(BF16)
                high_real, high_imag = dyson(br, bi, kr, ki)
                dressed_out[s, i, 0] = (low_real - high_real).astype(BF16)
                dressed_out[s, i, 1] = (low_imag + high_imag).astype(BF16)

                def part(d):
                    b, device = ka_peer(d)
                    send(
                        dressed_out.at[s, i, :, block_rows(b), :],
                        dressed_in.at[turn, s, own_column(s) * C + my_c, i],
                        dressed_sems.at[turn, s], device,
                    )

                loop(KA, part)
                return c

            lax.fori_loop(0, 2, one, 0)
            dressed_in[turn, s, own_column(s) * C + my_c] = dressed_out[s, :, :, my_rows, :]

        def to_times(s):
            take(dressed_in.at[turn, s, pl.ds(0, KA - 1)], dressed_sems.at[turn, s, 1])
            for uh in range(2):
                rows = pl.ds(uh * 16, 16)
                block = dressed_in[turn, s, :, :, :, rows, :].reshape(512, NO)
                value = mul(to_time[...], block).astype(BF16)
                time_out[s, :, rows, :] = value.reshape(TAU, 16, NO)

            def part(d):
                n, device = tau_peer(d)
                send(time_out.at[s, n], time_in.at[turn, s, t], time_sems.at[turn, s], device)

            loop(TAU, part)
            time_in[turn, s, t] = time_out[s, t]

        def finish(s):
            take(time_in.at[turn, s, pl.ds(0, TAU - 1)], time_sems.at[turn, s, 1])

            def place(b, j):
                return (lax.rem(b, C) * JUMP + j) * X + lax.rem(b // C + j + s, X)

            def part(d):
                b, device = ka_peer(d)
                for j in range(JUMP):
                    send(
                        time_in.at[turn, s, place(b, j)], home.at[turn, j, s, my_rows, :],
                        home_sems.at[turn, s], device,
                    )

            loop(KA, part)
            for j in range(JUMP):
                home[turn, j, s, my_rows, :] = time_in[turn, s, place(a, j)]
            for zh in range(2):
                for uh in range(2):
                    rows, points = pl.ds(uh * 16, 16), pl.ds(zh * 16, 16)
                    value = turn_over(swap, time_in[turn, s, points, rows, :])
                    old = x[turn, s, rows, points, :].astype(F32)
                    if turn == 0:
                        y[s, rows, points, :] = value
                        x[1, s, rows, points, :] = ((old + value.astype(F32)) * 0.5).astype(BF16)
                    else:
                        begin = x[0, s, rows, points, :].astype(F32)
                        first = y[s, rows, points, :].astype(F32) - begin
                        second = value.astype(F32) - old
                        for j, term in enumerate((first * first, first * second, second * second)):
                            partial[j] += jnp.sum(term.reshape(32, 8, NO), axis=0)

        to_frequencies(0)
        to_frequencies(1)
        solve(0)
        to_frequencies(2)
        to_times(0)
        solve(1)
        to_times(1)
        solve(2)
        to_times(2)
        for s in range(STEPS):
            finish(s)

    partial[...] = jnp.zeros_like(partial)
    one_round(0)
    one_round(1)

    index = lax.broadcasted_iota(jnp.int32, (8, 128), 0)
    tile = jnp.zeros((8, 128), F32)
    for j in range(3):
        line = jnp.sum(partial[j], axis=0, keepdims=True)
        line = line[:, :128] + line[:, 128:]
        tile = jnp.where(index == j, jnp.broadcast_to(line, (8, 128)), tile)
    sums[...] = tile
    loop(TAU, lambda d: send(sums, tau_sums.at[t], sum_sems.at[0], tau_peer(d)[1]))
    tau_sums[t] = tile
    take(tau_sums.at[pl.ds(0, TAU - 1)], sum_sems.at[0, 1])
    part_sums[...] = jnp.sum(tau_sums[...], axis=0)
    loop(KA, lambda d: send(part_sums, ka_sums.at[a], sum_sems.at[1], ka_peer(d)[1]))
    ka_sums[a] = part_sums[...]
    take(ka_sums.at[pl.ds(0, KA - 1)], sum_sems.at[1, 1])
    whole = jnp.sum(ka_sums[...], axis=0)
    means = [
        jnp.sum(jnp.where(index == j, whole, 0.0)) * (1.0 / (TAU * COUNT * NO * NO))
        for j in range(3)
    ]
    top = jnp.full((NO, NO), means[2] - means[1], F32)
    weight = top / (means[0] - 2.0 * means[1] + means[2] + 1e-06)
    rest = 1.0 - weight
    for s in range(STEPS):
        for turn in range(2):
            take(x_parts.at[s, pl.ds(0, KA - 1)], home_sems.at[turn, s, 1])
        for j in range(JUMP):
            value = weight * home[0, j, s].astype(F32) + rest * home[1, j, s].astype(F32)
            out[j, s] = value.astype(BF16)

    for s in range(STEPS):
        take(x_parts.at[s, pl.ds(0, KA - 1)], x_sems.at[s, 0])
        for uh in range(2):
            take(sigma_in.at[1, s, uh, pl.ds(0, TAU - 1)], sigma_sems.at[1, s, uh, 0])
        take(dressed_in.at[1, s, pl.ds(0, KA - 1)], freq_sems.at[1, s, 0])
        take(dressed_in.at[1, s, pl.ds(0, KA - 1)], dressed_sems.at[1, s, 0])
        take(time_in.at[1, s, pl.ds(0, TAU - 1)], time_sems.at[1, s, 0])
        for turn in range(2):
            take(x_parts.at[s, pl.ds(0, KA - 1)], home_sems.at[turn, s, 0])
        for j in range(JUMP):

            @pl.when(jnp.logical_not(goal(j, s)[0]))
            def _():
                take(bare.at[j, s], leave_sems.at[s, j])

    take(tau_sums.at[pl.ds(0, TAU - 1)], sum_sems.at[0, 0])
    take(ka_sums.at[pl.ds(0, KA - 1)], sum_sems.at[1, 0])


def per_device(green_times, screened, bare_green):
    operands = [
        green_times.reshape(JUMP, STEPS, NO, NO),
        screened[0],
        bare_green.reshape(JUMP, STEPS, 2, NO, NO),
    ] + tables()
    buffer = lambda *s: pltpu.VMEM(s, BF16)
    floats = lambda *s: pltpu.VMEM(s, F32)
    dma = lambda *s: pltpu.SemaphoreType.DMA(s)
    whole = pl.BlockSpec(memory_space=VMEM)
    mixed = pl.pallas_call(
        kernel,
        out_shape=jax.ShapeDtypeStruct((JUMP, STEPS, NO, NO), BF16),
        in_specs=[whole, whole, pl.BlockSpec(memory_space=pl.ANY)] + [whole] * 5,
        out_specs=whole,
        scratch_shapes=[
            buffer(STEPS, KA, JUMP, SUB, NO),
            buffer(2, STEPS, SUB, TAU, NO),
            buffer(SUB, COUNT, NO),
            buffer(STEPS, SUB, TAU, NO),
            buffer(STEPS, SUB, TAU, NO),
            buffer(STEPS, 2, TAU, 16, NO),
            buffer(2, STEPS, 2, TAU, 16, NO),
            buffer(STEPS, 2, KA, 2, 2, 16, NO),
            buffer(2, STEPS, 2, 2, NO, NO),
            buffer(STEPS, 2, 2, NO, NO),
            buffer(2, STEPS, KA, 2, 2, SUB, NO),
            buffer(STEPS, TAU, SUB, NO),
            buffer(2, STEPS, TAU, SUB, NO),
            buffer(2, JUMP, STEPS, NO, NO),
            buffer(STEPS, 2, 2, 2, NO, NO),
            floats(3, 8, NO),
            floats(8, 128),
            floats(TAU, 8, 128),
            floats(8, 128),
            floats(KA, 8, 128),
            dma(STEPS, 2),
            dma(STEPS, 2, 2),
            dma(STEPS, JUMP),
            dma(2, STEPS, 2, 2),
            dma(2, STEPS, 2),
            dma(2, STEPS, 2),
            dma(2, STEPS, 2),
            dma(2, STEPS, 2),
            dma(2, 2),
        ],
        compiler_params=pltpu.CompilerParams(
            collective_id=0, has_side_effects=True, vmem_limit_bytes=LIMIT
        ),
    )(*operands)
    return mixed.reshape(green_times.shape)


def solution(mesh):
    return jax.shard_map(
        per_device,
        mesh=mesh,
        in_specs=(
            P("tau", "ka", None, None),
            P("tau", None, "ka", None),
            P("tau", "ka", None, None, None),
        ),
        out_specs=P("tau", "ka", None, None),
        check_vma=False,
    )
```
